1024 devices in a mesh: nodes: 128 (over y, z), feat: 8 (over x, core).
Axes of the slice: x: 4, y: 8, z: 16, core: 2. Of those that a mesh axis runs over, the one named last changes fastest.
Arguments:
- features: bfloat16 [131072, 128], P('nodes', 'feat'), may hold values from -6 to 6
- adjacency: bfloat16 [1024, 4, 128, 128], P('nodes'), may hold values from 0 to 1, as said below
- source_ids: int32 [1024, 4], P('nodes'), may hold values from 0 to 15, as said below
- counts: int32 [1024], P('nodes'), may hold values from 1 to 4, as said below
- send_lists: int32 [128, 4, 2], P('nodes'), may hold values from 0 to 7
- first_self: bfloat16 [128, 256], replicated, may hold values from -0.5 to 0.5
- first_neighbour: bfloat16 [128, 256], replicated, may hold values from -0.5 to 0.5
- second_self: bfloat16 [256, 256], replicated, may hold values from -0.375 to 0.375
- second_neighbour: bfloat16 [256, 256], replicated, may hold values from -0.375 to 0.375
- upstream: bfloat16 [131072, 256], P(('nodes', 'feat')), may hold values from -6 to 6
Outputs:
- activations: bfloat16 [131072, 256], P(('nodes', 'feat'))
- feature_grad: bfloat16 [131072, 128], P('nodes', 'feat')
- first_self_grad: float32 [128, 256], P('feat')
- first_neighbour_grad: float32 [128, 256], P('feat')
- second_self_grad: float32 [256, 256], P('feat')
- second_neighbour_grad: float32 [256, 256], P('feat')
The draws below stay inside these ranges and needn't reach their ends.
Inputs may be any that keep to these rules, and one draw needn't show every extreme that they name: Within one partition the live counts stay at or under a level of that partition; some block of some partition has all 4 slots live. `source_ids`: slot 0 of every block is live; every block a partition receives is named in slot 0 of one of its blocks. `adjacency`: in slot 0 every row has at least one 1.
All inputs are finite; a program needn't handle non-finite values.
Results may differ from the reference program's by a relative error of at most 0.018.
Values may be sent and summed in bfloat16 or wider, within the bound.
A program may use at most 32 MiB of HBM per device.

```python
import jax
import jax.numpy as jnp
from jax import lax

F_IN = 128
HID = 256
BS = 128
K = 4
NOFF = 4
HS = 2
NB = 8
BLOCKS = 1024
NODES = 131072
N_NODES = 128


def draw_adjacency(key, part):
    key = jax.random.fold_in(key, 11)
    edge_key, column_key = jax.random.split(key)
    edges = jax.random.randint(edge_key, (BLOCKS, K, BS, BS), 0, 32) == 0
    forced = jax.random.randint(column_key, (BLOCKS, 1, BS, 1), 0, BS)
    slot_zero = jnp.arange(K, dtype=jnp.int32)[None, :, None, None] == 0
    column_hit = jnp.arange(BS, dtype=jnp.int32)[None, None, None, :] == forced
    return (edges | slot_zero & column_hit).astype(jnp.float32).astype(jnp.bfloat16)


def draw_counts(key, part):
    key = jax.random.fold_in(key, 23)
    level_key, pick_key, count_key, place_key = jax.random.split(key, 4)
    part_count = BLOCKS // NB
    levels = jax.random.randint(level_key, (part_count,), 1, K + 1)
    chosen = jax.random.randint(pick_key, (), 0, part_count)
    levels = jnp.where(jnp.arange(part_count) == chosen, K, levels)
    drawn = jax.random.randint(count_key, (part_count, NB), 1, levels[:, None] + 1)
    full_place = jax.random.randint(place_key, (part_count, 1), 0, NB)
    drawn = jnp.where(jnp.arange(NB)[None, :] == full_place, levels[:, None], drawn)
    return drawn.reshape(BLOCKS).astype(jnp.int32)


def draw_source_ids(key, part):
    key = jax.random.fold_in(key, 37)
    id_key, order_key = jax.random.split(key)
    part_count = BLOCKS // NB
    halo_count = NOFF * HS
    drawn = jax.random.randint(id_key, (part_count, NB, K), 0, NB + halo_count)
    orders = jax.vmap(lambda sub_key: jax.random.permutation(sub_key, NB))(jax.random.split(order_key, part_count))
    first_slot = jnp.where(orders < halo_count, NB + orders, drawn[:, :, 0])
    drawn = drawn.at[:, :, 0].set(first_slot)
    return drawn.reshape(BLOCKS, K).astype(jnp.int32)


def with_ends(entries, key, low, top_value):
    extent = entries.shape
    place = [jax.random.randint(jax.random.fold_in(key, axis), (), 0, extent[axis]) for axis in range(len(extent))]
    entries = entries.at[tuple(place)].set(low)
    longest = extent.index(max(extent))
    place[longest] = (place[longest] + 1) % extent[longest]
    return entries.at[tuple(place)].set(top_value)


def block_scale(rng, shape, cuts, low, largest):
    loudness, own = 1.0, jax.random.fold_in(rng, 6)
    for axis_at, shards_of in cuts:
        steps = jnp.exp(jax.random.uniform(jax.random.fold_in(own, axis_at), (shards_of,), jnp.float32, low / len(cuts), largest / len(cuts)))
        loudness = loudness * jnp.repeat(steps, shape[axis_at] // shards_of).reshape([-1 if axis == axis_at else 1 for axis in range(len(shape))])
    return loudness


def noise(rng, shape, spread, most, cuts=(), kind=jnp.bfloat16):
    array = spread * jax.random.normal(rng, shape, jnp.float32)
    if cuts:
        array = array * block_scale(rng, shape, cuts, -0.22, 0.18)
    return jnp.clip(array, -most, most).astype(kind)


def setup_inputs(seed: int = 0) -> dict:
    key_of = jax.random.split(jax.random.key(seed), 11)
    features = noise(key_of[0], (NODES, F_IN), 1.0, 6.0, ((0, 128), (1, 8)))
    adjacency = draw_adjacency(jax.random.fold_in(key_of[10], 71), 0)
    source_ids = draw_source_ids(jax.random.fold_in(key_of[10], 71), 0)
    counts = draw_counts(jax.random.fold_in(key_of[10], 71), 0)
    send_lists = with_ends(jax.random.randint(key_of[4], (N_NODES, NOFF, HS), 0, NB), jax.random.fold_in(key_of[4], 1), 0, NB - 1).astype(jnp.int32)
    first_self = noise(key_of[5], (F_IN, HID), F_IN ** -0.5, 0.5)
    first_neighbour = noise(key_of[6], (F_IN, HID), F_IN ** -0.5, 0.5)
    second_self = noise(key_of[7], (HID, HID), HID ** -0.5, 0.375)
    second_neighbour = noise(key_of[8], (HID, HID), HID ** -0.5, 0.375)
    upstream = noise(key_of[9], (NODES, HID), 1.0, 6.0, ((0, 1024),))
    return {"features": features, "adjacency": adjacency, "source_ids": source_ids, "counts": counts, "send_lists": send_lists, "first_self": first_self, "first_neighbour": first_neighbour, "second_self": second_self, "second_neighbour": second_neighbour, "upstream": upstream}


OFFSETS = (1, -1, 2, -2)


def silu_slope(values):
    gate_value = jax.nn.sigmoid(values)
    return gate_value * (1.0 + values * (1.0 - gate_value))


def with_halo(blocks_all, send_lists):
    pieces = [blocks_all]
    for slot_index, offset in enumerate(OFFSETS):
        donor_part = jnp.roll(blocks_all, offset, axis=0)
        chosen = jnp.roll(send_lists[:, slot_index, :], offset, axis=0)
        pieces.append(jax.vmap(lambda source, wanted: source[wanted])(donor_part, chosen))
    return jnp.concatenate(pieces, axis=1)


def aggregate(features_all, adjacency_all, source_all, live_all, degree_all, send_lists):
    sources = with_halo(features_all, send_lists)

    def per_part(bundle):
        sources_one, adjacency_one, ids_one, live_one, degree_one = bundle
        picked = sources_one[ids_one].astype(jnp.float32) * live_one[:, :, None, None]
        weighted = jnp.einsum("bkrs,bksc->brc", adjacency_one.astype(jnp.float32), picked)
        return weighted / degree_one[:, :, None]

    return lax.map(per_part, (sources, adjacency_all, source_all, live_all, degree_all))


def spread_back(scaled_all, adjacency_all, source_all, live_all, send_lists):
    total_blocks = adjacency_all.shape[1]
    per_offset = send_lists.shape[2]
    total_src = total_blocks + len(OFFSETS) * per_offset

    def per_part(bundle):
        scaled_one, adjacency_one, ids_one, live_one = bundle
        products = jnp.einsum("bkrs,brc->bksc", adjacency_one.astype(jnp.float32), scaled_one.astype(jnp.float32))
        onehot = (ids_one[:, :, None] == jnp.arange(total_src, dtype=jnp.int32)[None, None, :]).astype(jnp.float32)
        onehot = onehot * live_one[:, :, None]
        return jnp.einsum("bkn,bksc->nsc", onehot, products, precision=lax.Precision.HIGHEST)

    summed = lax.map(per_part, (scaled_all, adjacency_all, source_all, live_all))
    local_part = summed[:, :total_blocks]
    for slot_index, offset in enumerate(OFFSETS):
        lower = total_blocks + slot_index * per_offset
        outgoing = summed[:, lower:lower + per_offset]
        outgoing = lax.optimization_barrier(outgoing.astype(jnp.bfloat16)).astype(jnp.float32)
        returned = jnp.roll(outgoing, -offset, axis=0)
        select = (send_lists[:, slot_index, :, None] == jnp.arange(total_blocks, dtype=jnp.int32)[None, None, :]).astype(jnp.float32)
        local_part = local_part + jnp.einsum("phn,phsc->pnsc", select, returned, precision=lax.Precision.HIGHEST)
    return local_part


def reference(features, adjacency, source_ids, counts, send_lists, first_self, first_neighbour, second_self, second_neighbour, upstream):
    part_count = N_NODES
    live = (jnp.arange(K, dtype=jnp.int32)[None, :] < counts[:, None]).astype(jnp.float32).reshape(part_count, NB, K)
    adjacency_all = adjacency.reshape(part_count, NB, K, BS, BS)
    source_all = source_ids.reshape(part_count, NB, K)
    degree = lax.map(lambda bundle: jnp.einsum("bkrs,bk->br", bundle[0].astype(jnp.float32), bundle[1]), (adjacency_all, live))
    degree_rows = degree.reshape(NODES, 1)

    agg_one = aggregate(features.reshape(part_count, NB, BS, F_IN), adjacency_all, source_all, live, degree, send_lists)
    agg_one = agg_one.astype(jnp.bfloat16).reshape(NODES, F_IN)
    first_pre = jnp.dot(features, first_self, preferred_element_type=jnp.float32) + jnp.dot(agg_one, first_neighbour, preferred_element_type=jnp.float32)
    hidden = jax.nn.silu(first_pre).astype(jnp.bfloat16)
    agg_two = aggregate(hidden.reshape(part_count, NB, BS, HID), adjacency_all, source_all, live, degree, send_lists)
    agg_two = agg_two.astype(jnp.bfloat16).reshape(NODES, HID)
    second_pre = jnp.dot(hidden, second_self, preferred_element_type=jnp.float32) + jnp.dot(agg_two, second_neighbour, preferred_element_type=jnp.float32)
    activations = jax.nn.silu(second_pre).astype(jnp.bfloat16)

    delta_two = (upstream.astype(jnp.float32) * silu_slope(second_pre)).astype(jnp.bfloat16)
    self_two = jnp.dot(delta_two, second_self.T, preferred_element_type=jnp.float32).astype(jnp.bfloat16)
    scaled_two = (jnp.dot(delta_two, second_neighbour.T, preferred_element_type=jnp.float32) / degree_rows).astype(jnp.bfloat16)
    spread_two = spread_back(scaled_two.reshape(part_count, NB, BS, HID), adjacency_all, source_all, live, send_lists).reshape(NODES, HID)
    hidden_grad = (self_two.astype(jnp.float32) + spread_two).astype(jnp.bfloat16)
    delta_one = (hidden_grad.astype(jnp.float32) * silu_slope(first_pre)).astype(jnp.bfloat16)
    self_one = jnp.dot(delta_one, first_self.T, preferred_element_type=jnp.float32).astype(jnp.bfloat16)
    scaled_one = (jnp.dot(delta_one, first_neighbour.T, preferred_element_type=jnp.float32) / degree_rows).astype(jnp.bfloat16)
    spread_one = spread_back(scaled_one.reshape(part_count, NB, BS, F_IN), adjacency_all, source_all, live, send_lists).reshape(NODES, F_IN)
    feature_grad = (self_one.astype(jnp.float32) + spread_one).astype(jnp.bfloat16)

    grad_scale = NODES ** -0.5
    first_self_grad = jnp.dot(features.T, delta_one, preferred_element_type=jnp.float32) * grad_scale
    first_neighbour_grad = jnp.dot(agg_one.T, delta_one, preferred_element_type=jnp.float32) * grad_scale
    second_self_grad = jnp.dot(hidden.T, delta_two, preferred_element_type=jnp.float32) * grad_scale
    second_neighbour_grad = jnp.dot(agg_two.T, delta_two, preferred_element_type=jnp.float32) * grad_scale
    return (activations, feature_grad, first_self_grad, first_neighbour_grad, second_self_grad, second_neighbour_grad)
```

```python
import functools
import math

import jax
import jax.numpy as jnp
from jax import lax
from jax.experimental import pallas as pl
from jax.experimental.pallas import tpu as pltpu
from jax.sharding import PartitionSpec as P

OFFSETS = (1, -1, 2, -2)
MESH = pl.DeviceIdType.MESH
F32, BF16 = jnp.float32, jnp.bfloat16
NN = (((1,), (0,)), ((), ()))
NT = (((1,), (1,)), ((), ()))


def mm(lhs, rhs, dims=NN):
    return lax.dot_general(lhs, rhs, dims, preferred_element_type=F32)


def slope_of(values, gate):
    return gate * (1.0 + values * (1.0 - gate))


def kernel(
    sizes,
    scale,
    meta,
    x_ref,
    adj,
    w1s,
    w1n,
    w2s,
    w2n,
    up,
    act_o,
    fg_o,
    g1s_o,
    g1n_o,
    g2s_o,
    g2n_o,
    w1c,
    w1t,
    w2t,
    up_t,
    rdeg,
    x_own,
    x_halo_out,
    src1,
    agg1_col,
    row1,
    slope1,
    row2,
    h_own,
    h_halo_out,
    src2,
    agg2_col,
    d2,
    self2,
    u2_row,
    u2_col,
    prod,
    part,
    back2_out,
    back2_in,
    sp2_col,
    sp2_row,
    d1,
    u1_row,
    u1_col,
    back1_out,
    back1_in,
    g2_out,
    g2_in,
    g2y_out,
    g2y_in,
    g2z_out,
    g2z_in,
    g2_all,
    g1_out,
    g1_in,
    g1y_out,
    g1y_in,
    g1z_out,
    g1z_in,
    g1_all,
    feat_send,
    feat_recv,
    halo_send,
    halo_recv,
    y_send,
    y_recv,
    z_send,
    z_recv,
):
    nodes, ny, nz, nf, nb, ns = sizes
    p = lax.axis_index("nodes")
    f = lax.axis_index("feat")
    y, z = p // nz, p % nz
    cols1, cols2 = x_own.shape[1], h_own.shape[1]
    hid = d2.shape[0]
    halo_blocks = x_halo_out.shape[1]
    total = nb + len(OFFSETS) * halo_blocks

    def feat_peer(k):
        return (p, (f + k) % nf)

    def node_peer(offset):
        return ((p + nodes + offset) % nodes, f)

    def y_peer(k):
        return (((y + k) % ny) * nz + z, f)

    def z_peer(k):
        return (y * nz + (z + k) % nz, f)

    barrier = pltpu.get_barrier_semaphore()
    peers = (
        [feat_peer(k) for k in range(1, nf)]
        + [node_peer(o) for o in OFFSETS]
        + [y_peer(k) for k in range(1, ny)]
        + [z_peer(k) for k in range(1, nz)]
    )
    for peer in peers:
        pl.semaphore_signal(barrier, inc=1, device_id=peer, device_id_type=MESH)

    sent = []

    def start(src, dst, ssem, rsem, peer):
        copy = pltpu.make_async_remote_copy(
            src_ref=src, dst_ref=dst, send_sem=ssem, recv_sem=rsem, device_id=peer, device_id_type=MESH
        )
        copy.start()
        sent.append(copy)
        return copy

    def feat_hop(hop, src_of, dst):
        copies = []
        for k in range(1, nf):
            g = (f + k) % nf
            copies.append(
                start(src_of(g), dst, feat_send.at[hop, k - 1], feat_recv.at[hop, k - 1], feat_peer(k))
            )
        return copies

    def halo_hop(hop, src, dst_of, sign):
        return [
            start(src.at[i], dst_of(i), halo_send.at[hop, i], halo_recv.at[hop, i], node_peer(sign * o))
            for i, o in enumerate(OFFSETS)
        ]

    def line_hop(hop, size, src_of, dst, sems, peer_of, me):
        return [
            start(src_of((me + k) % size), dst, sems[0].at[hop, k - 1], sems[1].at[hop, k - 1], peer_of(k))
            for k in range(1, size)
        ]

    def landed(copies):
        for copy in copies:
            copy.wait_recv()

    for b in range(nb):
        x_own[b] = x_ref[:, 128 * b : 128 * (b + 1)]
    for i in range(len(OFFSETS)):
        for h in range(halo_blocks):
            x_halo_out[i, h] = x_own[meta[nb * ns + i * halo_blocks + h]]
    src1[pl.ds(0, nb)] = x_own[...]
    src1[total] = jnp.zeros((cols1, 128), BF16)
    src2[total] = jnp.zeros((cols2, 128), BF16)
    row1[f] = x_own[f]

    pl.semaphore_wait(barrier, len(peers))

    halo1 = halo_hop(0, x_halo_out, lambda i: src1.at[pl.ds(nb + halo_blocks * i, halo_blocks)], 1)
    x_rows = feat_hop(0, lambda g: x_own.at[g], row1.at[f])

    for b in range(nb):
        ones = jnp.concatenate(
            [
                jnp.full((16, 128), jnp.where(meta[b * ns + j] < total, 1.0, 0.0), F32)
                for j in range(ns)
            ],
            1,
        ).astype(BF16)
        deg = sum(mm(ones[:, 128 * j : 128 * (j + 1)], adj[b, j], NT) for j in range(ns))
        rdeg[b] = 1.0 / deg[0:8]
    w1c[0 : w1s.shape[0]] = w1s[...]
    w1c[w1s.shape[0] :] = w1n[...]
    w1t[...] = w1c[...].T
    w2t[:, 0:hid] = w2s[...].T
    w2t[:, hid:] = w2n[...].T
    up_t[...] = up[...].T

    def aggregate(src, out):
        for b in range(nb):
            total_b = sum(mm(src[meta[b * ns + j]], adj[b, j], NT) for j in range(ns))
            out[b] = (total_b * rdeg[b][0:1]).astype(BF16)

    def products(u, lo, c):
        for b in range(nb):
            rows = u[b][lo : lo + c]
            for j in range(ns):
                prod[b * ns + j, 0:c] = mm(rows, adj[b, j])

    def target_sum(n, c):
        acc = jnp.zeros((c, 128), F32)
        for t in range(nb * ns):
            acc = acc + jnp.where(meta[t] == n, 1.0, 0.0) * prod[t, 0:c]
        return acc

    def halo_sums(out, c):
        def body(n, carry):
            out[n // halo_blocks, n % halo_blocks] = target_sum(nb + n, c).astype(BF16)
            return carry

        lax.fori_loop(0, len(OFFSETS) * halo_blocks, body, 0, unroll=True)

    def own_sums(c):
        def body(n, carry):
            part[n, 0:c] = target_sum(n, c)
            return carry

        lax.fori_loop(0, nb, body, 0, unroll=True)

    def with_returned(back, n, c):
        acc = part[n, 0:c]
        for i in range(len(OFFSETS)):
            for h in range(halo_blocks):
                here = jnp.where(meta[nb * ns + i * halo_blocks + h] == n, 1.0, 0.0)
                acc = acc + here * back[i, h].astype(F32)
        return acc

    landed(halo1)
    aggregate(src1, agg1_col)
    agg1_rows = feat_hop(1, lambda g: agg1_col.at[g], row1.at[nf + f])
    row1[nf + f] = agg1_col[f]
    landed(x_rows)
    landed(agg1_rows)
    first_pre = mm(w1t[...], row1[...].reshape(2 * nf * cols1, 128))
    gate = jax.nn.sigmoid(first_pre)
    row2[0:nf] = (first_pre * gate).astype(BF16).reshape(nf, cols2, 128)
    h_cols = feat_hop(2, lambda g: row2.at[g], h_own.at[f])
    h_own[f] = row2[f]
    slope1[...] = slope_of(first_pre, gate)

    landed(h_cols)
    for i in range(len(OFFSETS)):
        for h in range(halo_blocks):
            h_halo_out[i, h] = h_own[meta[nb * ns + i * halo_blocks + h]]
    halo2 = halo_hop(1, h_halo_out, lambda i: src2.at[pl.ds(nb + halo_blocks * i, halo_blocks)], 1)
    src2[pl.ds(0, nb)] = h_own[...]
    landed(halo2)
    aggregate(src2, agg2_col)
    agg2_rows = feat_hop(3, lambda g: agg2_col.at[g], row2.at[nf + f])
    row2[nf + f] = agg2_col[f]
    landed(agg2_rows)
    rows2 = row2[...].reshape(2 * hid, 128)
    second_pre = mm(w2t[...], rows2)
    gate = jax.nn.sigmoid(second_pre)
    delta_two = (up_t[...].astype(F32) * slope_of(second_pre, gate)).astype(BF16)
    d2[...] = delta_two
    own_rdeg = rdeg[f][0:1]
    u2_row[...] = (mm(w2n[...], delta_two) * own_rdeg).astype(BF16).reshape(nf, cols2, 128)
    u2_cols = feat_hop(4, lambda g: u2_row.at[g], u2_col.at[f])
    u2_col[f] = u2_row[f]

    grad2 = mm(rows2, delta_two, NT).astype(BF16)
    g2_out[:, 0:cols2] = grad2[0:hid].reshape(nf, cols2, hid)
    g2_out[:, cols2:] = grad2[hid:].reshape(nf, cols2, hid)
    g2_feat = feat_hop(5, lambda g: g2_out.at[g], g2_in.at[f])
    g2_in[f] = g2_out[f]
    self2[...] = mm(w2s[...], delta_two).astype(BF16)
    act_o[...] = (second_pre * gate).T.astype(BF16)

    landed(u2_cols)
    products(u2_col, 0, cols2)
    halo_sums(back2_out, cols2)
    back2 = halo_hop(2, back2_out, lambda i: back2_in.at[i], -1)
    own_sums(cols2)
    landed(back2)
    for n in range(nb):
        sp2_col[n] = with_returned(back2_in, n, cols2).astype(BF16)
    sp2_rows = feat_hop(6, lambda g: sp2_col.at[g], sp2_row.at[f])
    sp2_row[f] = sp2_col[f]

    landed(g2_feat)
    g2_sum = g2_in[0].astype(F32)
    for k in range(1, nf):
        g2_sum = g2_sum + g2_in[k].astype(F32)
    g2y_out[...] = g2_sum.reshape(g2y_out.shape)
    y_sems, z_sems = (y_send, y_recv), (z_send, z_recv)
    g2_y = line_hop(0, ny, lambda g: g2y_out.at[g], g2y_in.at[y], y_sems, y_peer, y)
    g2y_in[y] = g2y_out[y]

    landed(sp2_rows)
    hidden_grad = (
        self2[...].astype(F32) + sp2_row[...].reshape(hid, 128).astype(F32)
    ).astype(BF16)
    delta_one = (hidden_grad.astype(F32) * slope1[...]).astype(BF16)
    rows1 = row1[...].reshape(2 * nf * cols1, 128)
    grad1 = mm(rows1, delta_one, NT).astype(BF16)
    half = nf * cols1
    g1_out[:, 0:cols1] = grad1[0:half].reshape(nf, cols1, hid)
    g1_out[:, cols1:] = grad1[half:].reshape(nf, cols1, hid)
    g1_feat = feat_hop(7, lambda g: g1_out.at[g], g1_in.at[f])
    g1_in[f] = g1_out[f]
    back = mm(w1c[...], delta_one)
    u1_row[:, 0:cols1] = back[0:half].astype(BF16).reshape(nf, cols1, 128)
    u1_row[:, cols1:] = (back[half:] * own_rdeg).astype(BF16).reshape(nf, cols1, 128)
    u1_cols = feat_hop(8, lambda g: u1_row.at[g], u1_col.at[f])
    u1_col[f] = u1_row[f]

    landed(g2_y)
    g2z_out[...] = jnp.sum(g2y_in[...], 0)
    g2_z = line_hop(0, nz, lambda g: g2z_out, g2z_in.at[z], z_sems, z_peer, z)
    g2z_in[z] = g2z_out[...]

    landed(g1_feat)
    g1_sum = g1_in[0].astype(F32)
    for k in range(1, nf):
        g1_sum = g1_sum + g1_in[k].astype(F32)
    lanes = hid // 128
    for a in range(g1_sum.shape[0] // 8):
        for b in range(lanes):
            g1y_out[a * lanes + b] = g1_sum[8 * a : 8 * (a + 1), 128 * b : 128 * (b + 1)]
    g1_y = line_hop(1, ny, lambda g: g1y_out.at[g], g1y_in.at[y], y_sems, y_peer, y)
    g1y_in[y] = g1y_out[y]

    landed(u1_cols)
    products(u1_col, cols1, cols1)
    halo_sums(back1_out, cols1)
    back1 = halo_hop(3, back1_out, lambda i: back1_in.at[i], -1)

    landed(g1_y)
    g1z_out[...] = jnp.sum(g1y_in[...], 0)
    g1_z = line_hop(1, nz, lambda g: g1z_out, g1z_in.at[z], z_sems, z_peer, z)
    g1z_in[z] = g1z_out[...]

    own_sums(cols1)

    landed(g2_z)
    g2_all[y] = jnp.sum(g2z_in[...], 0) * scale
    g2_back = line_hop(2, ny, lambda g: g2_all.at[y], g2_all.at[y], y_sems, y_peer, y)

    landed(back1)
    for n in range(nb):
        fg_o[:, 128 * n : 128 * (n + 1)] = (
            u1_col[n][0:cols1].astype(F32) + with_returned(back1_in, n, cols1)
        ).astype(BF16)

    landed(g1_z)
    g1_all[y] = jnp.sum(g1z_in[...], 0) * scale
    g1_back = line_hop(3, ny, lambda g: g1_all.at[y], g1_all.at[y], y_sems, y_peer, y)

    landed(g2_back)
    grads = g2_all[...].reshape(2 * cols2, hid)
    g2s_o[...] = grads[0:cols2]
    g2n_o[...] = grads[cols2:]

    landed(g1_back)
    for a in range(2 * cols1 // 8):
        for b in range(lanes):
            out = g1s_o if a < cols1 // 8 else g1n_o
            row = 8 * (a % (cols1 // 8))
            out[row : row + 8, 128 * b : 128 * (b + 1)] = g1_all[a * lanes + b]

    for copy in sent:
        copy.wait_send()


def on_device(
    features,
    adjacency,
    source_ids,
    counts,
    send_lists,
    first_self,
    first_neighbour,
    second_self,
    second_neighbour,
    upstream,
):
    nodes, nf = lax.axis_size("nodes"), lax.axis_size("feat")
    ny = 8
    nz = nodes // ny
    nb, ns, bs = adjacency.shape[0], adjacency.shape[1], adjacency.shape[2]
    hs = send_lists.shape[2]
    total = nb + len(OFFSETS) * hs
    c1 = features.shape[1]
    hid = upstream.shape[1]
    c2 = hid // nf
    live = jnp.arange(ns, dtype=jnp.int32)[None, :] < counts[:, None]
    meta = jnp.concatenate(
        [jnp.where(live, source_ids, total).reshape(-1), send_lists.reshape(-1)]
    )
    noff = len(OFFSETS)
    scale = 1.0 / math.sqrt(nb * bs * nodes)
    vmem = pl.BlockSpec(memory_space=pltpu.VMEM)
    scratch = [
        ((2 * nf * c1, hid), BF16),
        ((hid, 2 * nf * c1), BF16),
        ((hid, 2 * hid), BF16),
        ((hid, bs), BF16),
        ((nb, 8, bs), F32),
        ((nb, c1, bs), BF16),
        ((noff, hs, c1, bs), BF16),
        ((total + 1, c1, bs), BF16),
        ((nb, c1, bs), BF16),
        ((2 * nf, c1, bs), BF16),
        ((hid, bs), F32),
        ((2 * nf, c2, bs), BF16),
        ((nb, c2, bs), BF16),
        ((noff, hs, c2, bs), BF16),
        ((total + 1, c2, bs), BF16),
        ((nb, c2, bs), BF16),
        ((hid, bs), BF16),
        ((hid, bs), BF16),
        ((nf, c2, bs), BF16),
        ((nb, c2, bs), BF16),
        ((nb * ns, c2, bs), F32),
        ((nb, c2, bs), F32),
        ((noff, hs, c2, bs), BF16),
        ((noff, hs, c2, bs), BF16),
        ((nb, c2, bs), BF16),
        ((nf, c2, bs), BF16),
        ((hid, bs), BF16),
        ((nf, 2 * c1, bs), BF16),
        ((nb, 2 * c1, bs), BF16),
        ((noff, hs, c1, bs), BF16),
        ((noff, hs, c1, bs), BF16),
        ((nf, 2 * c2, hid), BF16),
        ((nf, 2 * c2, hid), BF16),
        ((ny, 2 * c2 // ny, hid), F32),
        ((ny, 2 * c2 // ny, hid), F32),
        ((2 * c2 // ny, hid), F32),
        ((nz, 2 * c2 // ny, hid), F32),
        ((ny, 2 * c2 // ny, hid), F32),
        ((nf, 2 * c1, hid), BF16),
        ((nf, 2 * c1, hid), BF16),
        ((ny, 8, 128), F32),
        ((ny, 8, 128), F32),
        ((8, 128), F32),
        ((nz, 8, 128), F32),
        ((ny, 8, 128), F32),
    ]
    dma = pltpu.SemaphoreType.DMA
    outs = pl.pallas_call(
        functools.partial(kernel, (nodes, ny, nz, nf, nb, ns), scale),
        out_shape=(
            jax.ShapeDtypeStruct((bs, hid), BF16),
            jax.ShapeDtypeStruct((c1, nb * bs), BF16),
            jax.ShapeDtypeStruct((c1, hid), F32),
            jax.ShapeDtypeStruct((c1, hid), F32),
            jax.ShapeDtypeStruct((c2, hid), F32),
            jax.ShapeDtypeStruct((c2, hid), F32),
        ),
        in_specs=[pl.BlockSpec(memory_space=pltpu.SMEM)] + [vmem] * 7,
        out_specs=(vmem,) * 6,
        scratch_shapes=[pltpu.VMEM(shape, kind) for shape, kind in scratch]
        + [
            dma((9, nf - 1)),
            dma((9, nf - 1)),
            dma((4, noff)),
            dma((4, noff)),
            dma((4, ny - 1)),
            dma((4, ny - 1)),
            dma((2, nz - 1)),
            dma((2, nz - 1)),
        ],
        compiler_params=pltpu.CompilerParams(
            collective_id=0, has_side_effects=True, vmem_limit_bytes=32 * 1024 * 1024
        ),
    )(
        meta,
        features.T,
        adjacency,
        first_self,
        first_neighbour,
        second_self,
        second_neighbour,
        upstream,
    )
    return (outs[0], outs[1].T) + tuple(outs[2:])


def solution(mesh):
    return jax.shard_map(
        on_device,
        mesh=mesh,
        in_specs=(
            P("nodes", "feat"),
            P("nodes", None, None, None),
            P("nodes", None),
            P("nodes"),
            P("nodes", None, None),
            P(),
            P(),
            P(),
            P(),
            P(("nodes", "feat"), None),
        ),
        out_specs=(
            P(("nodes", "feat"), None),
            P("nodes", "feat"),
            P("feat", None),
            P("feat", None),
            P("feat", None),
            P("feat", None),
        ),
        check_vma=False,
    )
```

```python
import functools
import math

import jax
import jax.numpy as jnp
from jax import lax
from jax.experimental import pallas as pl
from jax.experimental.pallas import tpu as pltpu
from jax.sharding import PartitionSpec as P

OFFSETS = (1, -1, 2, -2)
MESH = pl.DeviceIdType.MESH
F32, BF16 = jnp.float32, jnp.bfloat16
NN = (((1,), (0,)), ((), ()))
NT = (((1,), (1,)), ((), ()))


def mm(lhs, rhs, dims=NN):
    return lax.dot_general(lhs, rhs, dims, preferred_element_type=F32)


def slope_of(values, gate):
    return gate * (1.0 + values * (1.0 - gate))


def kernel(
    sizes,
    scale,
    ids_in,
    counts_in,
    lists_in,
    x_in,
    adj_in,
    w1s_in,
    w1n_in,
    w2s_in,
    w2n_in,
    up_in,
    act_out,
    fg_out,
    g1s_out,
    g1n_out,
    g2s_out,
    g2n_out,
    act_o,
    fg_o,
    g1s_o,
    g1n_o,
    g2s_o,
    g2n_o,
    ids,
    counts,
    lists,
    x_ref,
    adj,
    w1s,
    w1n,
    w2s,
    w2n,
    up,
    w1i,
    w1t,
    w2t,
    up_t,
    rdeg,
    x_own,
    x_halo_out,
    src1,
    agg1_col,
    r1,
    slope1,
    slope1_col,
    row2,
    h_own,
    h_halo_out,
    src2,
    agg2_col,
    d2,
    self2,
    u2_row,
    u2_col,
    prod,
    part,
    back2_out,
    back2_in,
    sp2_col,
    sp2_row,
    u1_row,
    u1_col,
    back1_out,
    back1_in,
    g2_out,
    g2_in,
    g2y_out,
    g2y_in,
    g2z_out,
    g2z_in,
    g2_all,
    g1y_out,
    g1y_in,
    g1z_out,
    g1z_in,
    g1_own,
    g1_all,
    feat_send,
    feat_recv,
    halo_send,
    halo_recv,
    y_send,
    y_recv,
    z_send,
    z_recv,
    cross_send,
    cross_recv,
    load_sems,
    store_sems,
):
    nodes, ny, nz, nf, nb, ns = sizes
    p = lax.axis_index("nodes")
    f = lax.axis_index("feat")
    y, z = p // nz, p % nz
    cols1, cols2 = x_own.shape[1], h_own.shape[1]
    hid = d2.shape[0]
    halo_blocks = x_halo_out.shape[1]
    total = nb + len(OFFSETS) * halo_blocks

    def feat_peer(k):
        return (p, (f + k) % nf)

    def node_peer(offset):
        return ((p + nodes + offset) % nodes, f)

    def y_peer(k):
        return (((y + k) % ny) * nz + z, f)

    def z_peer(k):
        return (y * nz + (z + k) % nz, f)

    def far_first(size):
        return sorted(range(1, size), key=lambda k: -min(k, size - k))

    loads = [
        pltpu.make_async_copy(src, dst, load_sems.at[i])
        for i, (src, dst) in enumerate(
            (
                (x_in, x_ref),
                (lists_in, lists),
                (ids_in, ids),
                (counts_in, counts),
                (adj_in, adj),
                (w1s_in, w1s),
                (w1n_in, w1n),
                (w2s_in, w2s),
                (w2n_in, w2n),
                (up_in, up),
            )
        )
    ]
    for load in loads:
        load.start()
    stores = [
        pltpu.make_async_copy(src, dst, store_sems.at[i])
        for i, (src, dst) in enumerate(
            (
                (act_o, act_out),
                (fg_o, fg_out),
                (g1s_o, g1s_out),
                (g1n_o, g1n_out),
                (g2s_o, g2s_out),
                (g2n_o, g2n_out),
            )
        )
    ]

    barrier = pltpu.get_barrier_semaphore()
    peers = (
        [feat_peer(k) for k in range(1, nf)]
        + [node_peer(o) for o in OFFSETS]
        + [y_peer(k) for k in range(1, ny)]
        + [z_peer(k) for k in range(1, nz)]
    )
    for peer in peers:
        pl.semaphore_signal(barrier, inc=1, device_id=peer, device_id_type=MESH)
    for s in range(nf):

        @pl.when(jnp.logical_or(f != y, f != s))
        def _():
            pl.semaphore_signal(barrier, inc=1, device_id=(f * nz + z, s), device_id_type=MESH)

    arrivals = len(peers) + ny - jnp.where(f == y, 1, 0)

    sent = []

    def start(src, dst, ssem, rsem, peer):
        copy = pltpu.make_async_remote_copy(
            src_ref=src, dst_ref=dst, send_sem=ssem, recv_sem=rsem, device_id=peer, device_id_type=MESH
        )
        copy.start()
        sent.append(copy)
        return copy

    def feat_hop(hop, src_of, dst):
        copies = []
        for k in far_first(nf):
            g = (f + k) % nf
            copies.append(
                start(src_of(g), dst, feat_send.at[hop, k - 1], feat_recv.at[hop, k - 1], feat_peer(k))
            )
        return copies

    def halo_hop(hop, src, dst_of, sign):
        return [
            start(src.at[i], dst_of(i), halo_send.at[hop, i], halo_recv.at[hop, i], node_peer(sign * o))
            for i, o in sorted(enumerate(OFFSETS), key=lambda pair: -abs(pair[1]))
        ]

    def line_hop(hop, size, src_of, dst, sems, peer_of, me):
        return [
            start(src_of((me + k) % size), dst, sems[0].at[hop, k - 1], sems[1].at[hop, k - 1], peer_of(k))
            for k in far_first(size)
        ]

    def landed(copies):
        for copy in copies:
            copy.wait_recv()

    loads[0].wait()
    loads[1].wait()
    sent_ids = [[lists[0, h, i] for h in range(halo_blocks)] for i in range(len(OFFSETS))]
    for b in range(nb):
        x_own[b] = x_ref[:, 128 * b : 128 * (b + 1)]
    for i in range(len(OFFSETS)):
        for h in range(halo_blocks):
            x_halo_out[i, h] = x_own[sent_ids[i][h]]

    pl.semaphore_wait(barrier, arrivals)

    halo1 = halo_hop(0, x_halo_out, lambda i: src1.at[pl.ds(nb + halo_blocks * i, halo_blocks)], 1)
    x_all = feat_hop(0, lambda g: x_own, r1.at[:, f, 0])

    src1[pl.ds(0, nb)] = x_own[...]
    src1[total] = jnp.zeros((cols1, 128), BF16)
    src2[total] = jnp.zeros((cols2, 128), BF16)
    r1[:, f, 0] = x_own[...]
    for load in loads[2:5]:
        load.wait()
    targets = [
        [jnp.where(j < counts[b], ids[j, b], total) for j in range(ns)] for b in range(nb)
    ]
    flat_targets = [t for of_block in targets for t in of_block]
    for b in range(nb):
        ones = jnp.concatenate(
            [
                jnp.full((16, 128), jnp.where(targets[b][j] < total, 1.0, 0.0), F32)
                for j in range(ns)
            ],
            1,
        ).astype(BF16)
        deg = sum(mm(ones[:, 128 * j : 128 * (j + 1)], adj[b, j], NT) for j in range(ns))
        rdeg[b] = 1.0 / deg[0:8]
    for load in loads[5:]:
        load.wait()
    for g in range(nf):
        w1i[g, 0:cols1] = w1s[cols1 * g : cols1 * (g + 1)]
        w1i[g, cols1:] = w1n[cols1 * g : cols1 * (g + 1)]
    w1t[...] = w1i[...].reshape(2 * nf * cols1, hid).T.reshape(w1t.shape)
    w2t[:, 0:hid] = w2s[...].T
    w2t[:, hid:] = w2n[...].T
    up_t[...] = up[...].T

    def aggregate(src, out):
        for b in range(nb):
            total_b = sum(mm(src[targets[b][j]], adj[b, j], NT) for j in range(ns))
            out[b] = (total_b * rdeg[b][0:1]).astype(BF16)

    def products(u, lo, c):
        for b in range(nb):
            rows = u[b][lo : lo + c]
            for j in range(ns):
                prod[b * ns + j, 0:c] = mm(rows, adj[b, j])

    def target_sum(n, c):
        acc = jnp.zeros((c, 128), F32)
        for t in range(nb * ns):
            acc = acc + jnp.where(flat_targets[t] == n, 1.0, 0.0) * prod[t, 0:c]
        return acc

    def halo_sums(out, c):
        def body(n, carry):
            out[n // halo_blocks, n % halo_blocks] = target_sum(nb + n, c).astype(BF16)
            return carry

        lax.fori_loop(0, len(OFFSETS) * halo_blocks, body, 0, unroll=True)

    def own_sums(c):
        def body(n, carry):
            part[n, 0:c] = target_sum(n, c)
            return carry

        lax.fori_loop(0, nb, body, 0, unroll=True)

    def with_returned(back, n, c):
        acc = part[n, 0:c]
        for i in range(len(OFFSETS)):
            for h in range(halo_blocks):
                here = jnp.where(sent_ids[i][h] == n, 1.0, 0.0)
                acc = acc + here * back[i, h].astype(F32)
        return acc

    landed(halo1)
    aggregate(src1, agg1_col)
    agg1_all = feat_hop(1, lambda g: agg1_col, r1.at[:, f, 1])
    r1[:, f, 1] = agg1_col[...]
    landed(x_all)
    landed(agg1_all)
    blocks1 = [r1[b].reshape(2 * nf * cols1, 128) for b in range(nb)]
    first_cols = mm(w1t[f], jnp.concatenate(blocks1, 1))
    gate = jax.nn.sigmoid(first_cols)
    hidden_cols = (first_cols * gate).astype(BF16)
    for b in range(nb):
        h_own[b] = hidden_cols[:, 128 * b : 128 * (b + 1)]
    for i in range(len(OFFSETS)):
        for h in range(halo_blocks):
            h_halo_out[i, h] = h_own[sent_ids[i][h]]
    halo2 = halo_hop(1, h_halo_out, lambda i: src2.at[pl.ds(nb + halo_blocks * i, halo_blocks)], 1)
    slope1_col[...] = slope_of(first_cols, gate)
    first_pre = mm(w1t[...].reshape(hid, 2 * nf * cols1), r1[f].reshape(2 * nf * cols1, 128))
    gate = jax.nn.sigmoid(first_pre)
    row2[0:nf] = (first_pre * gate).astype(BF16).reshape(nf, cols2, 128)
    slope1[...] = slope_of(first_pre, gate)

    src2[pl.ds(0, nb)] = h_own[...]
    landed(halo2)
    aggregate(src2, agg2_col)
    agg2_rows = feat_hop(2, lambda g: agg2_col.at[g], row2.at[nf + f])
    row2[nf + f] = agg2_col[f]
    landed(agg2_rows)
    rows2 = row2[...].reshape(2 * hid, 128)
    second_pre = mm(w2t[...], rows2)
    gate = jax.nn.sigmoid(second_pre)
    delta_two = (up_t[...].astype(F32) * slope_of(second_pre, gate)).astype(BF16)
    d2[...] = delta_two
    own_rdeg = rdeg[f][0:1]
    u2_row[:, 0:cols2] = (mm(w2n[...], delta_two) * own_rdeg).astype(BF16).reshape(nf, cols2, 128)
    self_two = mm(w2s[...], delta_two).astype(BF16)
    self2[...] = self_two
    u2_row[:, cols2:] = self_two.reshape(nf, cols2, 128)
    u2_cols = feat_hop(3, lambda g: u2_row.at[g], u2_col.at[f])
    u2_col[f] = u2_row[f]

    grad2 = mm(rows2, delta_two, NT).astype(BF16)
    g2_out[:, 0:cols2] = grad2[0:hid].reshape(nf, cols2, hid)
    g2_out[:, cols2:] = grad2[hid:].reshape(nf, cols2, hid)
    g2_feat = feat_hop(4, lambda g: g2_out.at[g], g2_in.at[f])
    g2_in[f] = g2_out[f]
    act_o[...] = (second_pre * gate).T.astype(BF16)
    stores[0].start()

    landed(u2_cols)
    products(u2_col, 0, cols2)
    halo_sums(back2_out, cols2)
    back2 = halo_hop(2, back2_out, lambda i: back2_in.at[i], -1)
    own_sums(cols2)
    landed(g2_feat)
    g2_sum = g2_in[0].astype(F32)
    for k in range(1, nf):
        g2_sum = g2_sum + g2_in[k].astype(F32)
    g2y_out[...] = g2_sum.reshape(g2y_out.shape)
    y_sems, z_sems = (y_send, y_recv), (z_send, z_recv)
    g2_y = line_hop(0, ny, lambda g: g2y_out.at[g], g2y_in.at[y], y_sems, y_peer, y)
    g2y_in[y] = g2y_out[y]

    landed(back2)
    grad1 = jnp.zeros((cols2, 2 * nf * cols1), F32)
    for n in range(nb):
        spread_two = with_returned(back2_in, n, cols2)
        sp2_col[n] = spread_two.astype(BF16)
        hidden_grad = (u2_col[n][cols2:].astype(F32) + spread_two).astype(BF16)
        slopes = slope1_col[:, 128 * n : 128 * (n + 1)]
        delta_cols = (hidden_grad.astype(F32) * slopes).astype(BF16)
        grad1 = grad1 + mm(delta_cols, r1[n].reshape(2 * nf * cols1, 128), NT)
    group = lax.broadcasted_iota(jnp.int32, (8, 128), 1) // (2 * cols1)
    for g in range(nf):
        lane = 2 * cols1 * g
        wide = grad1[:, lane // 128 * 128 : lane // 128 * 128 + 128]
        packed = jnp.zeros((8, 128), F32)
        for q in range(128 // (2 * cols1)):
            shift = (2 * cols1 * q - lane) % 128
            piece = wide[8 * q : 8 * (q + 1)]
            packed = jnp.where(group == q, pltpu.roll(piece, shift, 1) if shift else piece, packed)
        g1y_out[g] = packed
    g1_y = line_hop(1, ny, lambda g: g1y_out.at[g], g1y_in.at[y], y_sems, y_peer, y)
    g1y_in[y] = g1y_out[y]
    sp2_rows = feat_hop(5, lambda g: sp2_col.at[g], sp2_row.at[f])
    sp2_row[f] = sp2_col[f]

    landed(g2_y)
    g2_chunk = jnp.sum(g2y_in[...], 0)
    for a in range(hid // 128):
        g2z_out[8 * a : 8 * (a + 1)] = g2_chunk[:, 128 * a : 128 * (a + 1)].astype(BF16)
    g2_z = line_hop(0, nz, lambda g: g2z_out, g2z_in.at[z], z_sems, z_peer, z)
    g2z_in[z] = g2z_out[...]

    landed(sp2_rows)
    hidden_grad = (
        self2[...].astype(F32) + sp2_row[...].reshape(hid, 128).astype(F32)
    ).astype(BF16)
    delta_one = (hidden_grad.astype(F32) * slope1[...]).astype(BF16)
    back = mm(w1i[...].reshape(2 * nf * cols1, hid), delta_one).reshape(nf, 2 * cols1, 128)
    u1_row[:, 0:cols1] = back[:, 0:cols1].astype(BF16)
    u1_row[:, cols1:] = (back[:, cols1:] * own_rdeg).astype(BF16)
    u1_cols = feat_hop(6, lambda g: u1_row.at[g], u1_col.at[f])
    u1_col[f] = u1_row[f]

    landed(g1_y)
    g1z_out[...] = jnp.sum(g1y_in[...], 0)
    g1_z = line_hop(1, nz, lambda g: g1z_out, g1z_in.at[z], z_sems, z_peer, z)
    g1z_in[z] = g1z_out[...]

    landed(u1_cols)
    products(u1_col, cols1, cols1)
    halo_sums(back1_out, cols1)
    back1 = halo_hop(3, back1_out, lambda i: back1_in.at[i], -1)
    own_sums(cols1)

    landed(g2_z)
    g2_final = jnp.sum(g2z_in[...].astype(F32), 0) * scale
    for a in range(hid // 128):
        g2_all[y, :, 128 * a : 128 * (a + 1)] = g2_final[8 * a : 8 * (a + 1)]
    g2_back = line_hop(2, ny, lambda g: g2_all.at[y], g2_all.at[y], y_sems, y_peer, y)

    landed(g1_z)
    g1_own[...] = jnp.sum(g1z_in[...], 0) * scale
    cross = [
        pltpu.make_async_remote_copy(
            src_ref=g1_own,
            dst_ref=g1_all.at[f],
            send_sem=cross_send.at[k],
            recv_sem=cross_recv.at[f],
            device_id=(((y + k) % ny) * nz + z, y),
            device_id_type=MESH,
        )
        for k in range(ny)
    ]
    for k in far_first(ny):
        cross[k].start()

    @pl.when(f != y)
    def _():
        cross[0].start()

    @pl.when(f == y)
    def _():
        g1_all[f] = g1_own[...]

    landed(back1)
    for n in range(nb):
        fg_o[:, 128 * n : 128 * (n + 1)] = (
            u1_col[n][0:cols1].astype(F32) + with_returned(back1_in, n, cols1)
        ).astype(BF16)
    stores[1].start()

    landed(g2_back)
    grads = g2_all[...].reshape(2 * cols2, hid)
    g2s_o[...] = grads[0:cols2]
    g2n_o[...] = grads[cols2:]
    stores[4].start()
    stores[5].start()

    for s in range(nf):

        @pl.when(jnp.logical_or(f != y, f != s))
        def _():
            pltpu.make_async_remote_copy(
                src_ref=g1_own,
                dst_ref=g1_all.at[s],
                send_sem=cross_send.at[0],
                recv_sem=cross_recv.at[s],
                device_id=(f * nz + z, s),
                device_id_type=MESH,
            ).wait_recv()

    tiles = []
    for s in range(nf):
        tile = g1_all[s]
        for q in range(128 // (2 * cols1)):
            tiles.append(pltpu.roll(tile, 128 - 2 * cols1 * q, 1) if q else tile)
    grad1_rows = jnp.concatenate(tiles, 0).T
    g1s_o[...] = grad1_rows[0:cols1]
    g1n_o[...] = grad1_rows[cols1 : 2 * cols1]
    stores[2].start()
    stores[3].start()

    for k in range(1, ny):
        cross[k].wait_send()

    @pl.when(f != y)
    def _():
        cross[0].wait_send()

    for copy in sent:
        copy.wait_send()
    for copy in stores:
        copy.wait()


def store(count, *refs):
    ins, outs, held = refs[:count], refs[count : 2 * count], refs[2 * count : 3 * count]
    sems = refs[-1]
    fetch = [pltpu.make_async_copy(ins[i], held[i], sems.at[0, i]) for i in range(count)]
    write = [pltpu.make_async_copy(held[i], outs[i], sems.at[1, i]) for i in range(count)]
    for copy in fetch:
        copy.start()
    for first, second in zip(fetch, write):
        first.wait()
        second.start()
    for copy in write:
        copy.wait()


def on_device(
    features,
    adjacency,
    source_ids,
    counts,
    send_lists,
    first_self,
    first_neighbour,
    second_self,
    second_neighbour,
    upstream,
):
    nodes, nf = lax.axis_size("nodes"), lax.axis_size("feat")
    ny = 8
    nz = nodes // ny
    nb, ns, bs = adjacency.shape[0], adjacency.shape[1], adjacency.shape[2]
    hs = send_lists.shape[2]
    total = nb + len(OFFSETS) * hs
    c1 = features.shape[1]
    hid = upstream.shape[1]
    c2 = hid // nf
    noff = len(OFFSETS)
    scale = 1.0 / math.sqrt(nb * bs * nodes)
    hbm = pl.BlockSpec(memory_space=pltpu.HBM)
    scratch = [
        ((bs, hid), BF16),
        ((c1, nb * bs), BF16),
        ((c1, hid), F32),
        ((c1, hid), F32),
        ((c2, hid), F32),
        ((c2, hid), F32),
        ((c1, nb * bs), BF16),
        (adjacency.shape, BF16),
        (first_self.shape, BF16),
        (first_neighbour.shape, BF16),
        (second_self.shape, BF16),
        (second_neighbour.shape, BF16),
        (upstream.shape, BF16),
        ((nf, 2 * c1, hid), BF16),
        ((nf, c2, 2 * nf * c1), BF16),
        ((hid, 2 * hid), BF16),
        ((hid, bs), BF16),
        ((nb, 8, bs), F32),
        ((nb, c1, bs), BF16),
        ((noff, hs, c1, bs), BF16),
        ((total + 1, c1, bs), BF16),
        ((nb, c1, bs), BF16),
        ((nb, nf, 2, c1, bs), BF16),
        ((hid, bs), F32),
        ((c2, nb * bs), F32),
        ((2 * nf, c2, bs), BF16),
        ((nb, c2, bs), BF16),
        ((noff, hs, c2, bs), BF16),
        ((total + 1, c2, bs), BF16),
        ((nb, c2, bs), BF16),
        ((hid, bs), BF16),
        ((hid, bs), BF16),
        ((nf, 2 * c2, bs), BF16),
        ((nb, 2 * c2, bs), BF16),
        ((nb * ns, c2, bs), F32),
        ((nb, c2, bs), F32),
        ((noff, hs, c2, bs), BF16),
        ((noff, hs, c2, bs), BF16),
        ((nb, c2, bs), BF16),
        ((nf, c2, bs), BF16),
        ((nf, 2 * c1, bs), BF16),
        ((nb, 2 * c1, bs), BF16),
        ((noff, hs, c1, bs), BF16),
        ((noff, hs, c1, bs), BF16),
        ((nf, 2 * c2, hid), BF16),
        ((nf, 2 * c2, hid), BF16),
        ((ny, 2 * c2 // ny, hid), F32),
        ((ny, 2 * c2 // ny, hid), F32),
        ((16, 128), BF16),
        ((nz, 16, 128), BF16),
        ((ny, 2 * c2 // ny, hid), F32),
        ((ny, 8, 128), F32),
        ((ny, 8, 128), F32),
        ((8, 128), F32),
        ((nz, 8, 128), F32),
        ((8, 128), F32),
        ((nf, 8, 128), F32),
    ]
    dma = pltpu.SemaphoreType.DMA
    outs = pl.pallas_call(
        functools.partial(kernel, (nodes, ny, nz, nf, nb, ns), scale),
        out_shape=(
            jax.ShapeDtypeStruct((bs, hid), BF16),
            jax.ShapeDtypeStruct((c1, nb * bs), BF16),
            jax.ShapeDtypeStruct((c1, hid), F32),
            jax.ShapeDtypeStruct((c1, hid), F32),
            jax.ShapeDtypeStruct((c2, hid), F32),
            jax.ShapeDtypeStruct((c2, hid), F32),
        ),
        in_specs=[hbm] * 10,
        out_specs=(hbm,) * 6,
        scratch_shapes=[pltpu.VMEM(shape, kind) for shape, kind in scratch[:6]]
        + [
            pltpu.SMEM((ns, nb), jnp.int32),
            pltpu.SMEM((nb,), jnp.int32),
            pltpu.SMEM((1, hs, noff), jnp.int32),
        ]
        + [pltpu.VMEM(shape, kind) for shape, kind in scratch[6:]]
        + [
            dma((7, nf - 1)),
            dma((7, nf - 1)),
            dma((4, noff)),
            dma((4, noff)),
            dma((3, ny - 1)),
            dma((3, ny - 1)),
            dma((2, nz - 1)),
            dma((2, nz - 1)),
            dma((ny,)),
            dma((nf,)),
            dma((10,)),
            dma((6,)),
        ],
        compiler_params=pltpu.CompilerParams(
            collective_id=0, has_side_effects=True, vmem_limit_bytes=60 * 1024 * 1024
        ),
    )(
        source_ids.T,
        counts,
        send_lists.transpose(0, 2, 1),
        features.T,
        adjacency,
        first_self,
        first_neighbour,
        second_self,
        second_neighbour,
        upstream,
    )
    outs = pl.pallas_call(
        functools.partial(store, len(outs)),
        out_shape=tuple(jax.ShapeDtypeStruct(o.shape, o.dtype) for o in outs),
        in_specs=[hbm] * len(outs),
        out_specs=(hbm,) * len(outs),
        scratch_shapes=[pltpu.VMEM(o.shape, o.dtype) for o in outs] + [dma((2, len(outs)))],
        compiler_params=pltpu.CompilerParams(vmem_limit_bytes=60 * 1024 * 1024),
    )(*outs)
    return (outs[0], outs[1].T) + tuple(outs[2:])


def solution(mesh):
    return jax.shard_map(
        on_device,
        mesh=mesh,
        in_specs=(
            P("nodes", "feat"),
            P("nodes", None, None, None),
            P("nodes", None),
            P("nodes"),
            P("nodes", None, None),
            P(),
            P(),
            P(),
            P(),
            P(("nodes", "feat"), None),
        ),
        out_specs=(
            P(("nodes", "feat"), None),
            P("nodes", "feat"),
            P("feat", None),
            P("feat", None),
            P("feat", None),
            P("feat", None),
        ),
        check_vma=False,
    )
```

```python
import functools
import math

import jax
import jax.numpy as jnp
from jax import lax
from jax.experimental import pallas as pl
from jax.experimental.pallas import tpu as pltpu
from jax.sharding import PartitionSpec as P

OFFSETS = (1, -1, 2, -2)
MESH = pl.DeviceIdType.MESH
F32, BF16 = jnp.float32, jnp.bfloat16
NN = (((1,), (0,)), ((), ()))
NT = (((1,), (1,)), ((), ()))


def mm(lhs, rhs, dims=NN):
    return lax.dot_general(lhs, rhs, dims, preferred_element_type=F32)


def slope_of(values, gate):
    return gate * (1.0 + values * (1.0 - gate))


def kernel(
    sizes,
    scale,
    ids_in,
    counts_in,
    lists_in,
    x_in,
    adj_in,
    w1s_in,
    w1n_in,
    w2s_in,
    w2n_in,
    up_in,
    act_out,
    fg_out,
    g1s_out,
    g1n_out,
    g2s_out,
    g2n_out,
    act_o,
    fg_o,
    g1s_o,
    g1n_o,
    g2s_o,
    g2n_o,
    ids,
    counts,
    lists,
    x_ref,
    adj,
    w1s,
    w1n,
    w2s,
    w2n,
    up,
    w1i,
    w1t,
    w2t,
    up_t,
    rdeg,
    x_own,
    x_halo_out,
    src1,
    agg1_col,
    r1,
    slope1,
    slope1_col,
    slope_halo_out,
    slope_halo_in,
    r1_halo_out,
    r1_halo_in,
    row2,
    h_own,
    h_halo_out,
    src2,
    agg2_col,
    d2,
    self2,
    u2_row,
    u2_col,
    to_halo,
    to_own,
    part,
    back2_out,
    back2_in,
    sp2_col,
    sp2_row,
    u1_row,
    u1_col,
    back1_out,
    back1_in,
    g2_out,
    g2_in,
    g2y_out,
    g2y_in,
    g2z_out,
    g2z_in,
    g2_all,
    g1y_out,
    g1y_in,
    g1z_out,
    g1z_in,
    g1_own,
    g1_all,
    feat_send,
    feat_recv,
    halo_send,
    halo_recv,
    y_send,
    y_recv,
    z_send,
    z_recv,
    cross_send,
    cross_recv,
    load_sems,
    store_sems,
):
    nodes, ny, nz, nf, nb, ns = sizes
    p = lax.axis_index("nodes")
    f = lax.axis_index("feat")
    y, z = p // nz, p % nz
    cols1, cols2 = x_own.shape[1], h_own.shape[1]
    hid = d2.shape[0]
    halo_blocks = x_halo_out.shape[1]
    total = nb + len(OFFSETS) * halo_blocks

    def feat_peer(k):
        return (p, (f + k) % nf)

    def node_peer(offset):
        return ((p + nodes + offset) % nodes, f)

    def y_peer(k):
        return (((y + k) % ny) * nz + z, f)

    def z_peer(k):
        return (y * nz + (z + k) % nz, f)

    def far_first(size):
        return sorted(range(1, size), key=lambda k: -min(k, size - k))

    loads = [
        pltpu.make_async_copy(src, dst, load_sems.at[i])
        for i, (src, dst) in enumerate(
            (
                (x_in, x_ref),
                (lists_in, lists),
                (ids_in, ids),
                (counts_in, counts),
                (adj_in, adj),
                (w1s_in, w1s),
                (w1n_in, w1n),
                (w2s_in, w2s),
                (w2n_in, w2n),
                (up_in, up),
            )
        )
    ]
    for load in loads:
        load.start()
    stores = [
        pltpu.make_async_copy(src, dst, store_sems.at[i])
        for i, (src, dst) in enumerate(
            (
                (act_o, act_out),
                (fg_o, fg_out),
                (g1s_o, g1s_out),
                (g1n_o, g1n_out),
                (g2s_o, g2s_out),
                (g2n_o, g2n_out),
            )
        )
    ]

    barrier = pltpu.get_barrier_semaphore()
    peers = (
        [node_peer(o) for o in OFFSETS]
        + [feat_peer(k) for k in range(1, nf)]
        + [y_peer(k) for k in range(1, ny)]
        + [z_peer(k) for k in range(1, nz)]
    )
    for peer in peers:
        pl.semaphore_signal(barrier, inc=1, device_id=peer, device_id_type=MESH)
    for s in range(nf):

        @pl.when(jnp.logical_or(f != y, f != s))
        def _():
            pl.semaphore_signal(barrier, inc=1, device_id=(f * nz + z, s), device_id_type=MESH)

    arrivals = len(peers) + ny - jnp.where(f == y, 1, 0)

    sent = []

    def drain():
        while sent:
            sent.pop(0).wait_send()

    def start(src, dst, ssem, rsem, peer):
        copy = pltpu.make_async_remote_copy(
            src_ref=src, dst_ref=dst, send_sem=ssem, recv_sem=rsem, device_id=peer, device_id_type=MESH
        )
        copy.start()
        sent.append(copy)
        return copy

    def feat_hop(hop, src_of, dst):
        copies = []
        for k in far_first(nf):
            g = (f + k) % nf
            copies.append(
                start(src_of(g), dst, feat_send.at[hop, k - 1], feat_recv.at[hop, k - 1], feat_peer(k))
            )
        return copies

    def halo_hop(hop, src, dst_of, sign):
        return [
            start(src.at[i], dst_of(i), halo_send.at[hop, i], halo_recv.at[hop, i], node_peer(sign * o))
            for i, o in sorted(enumerate(OFFSETS), key=lambda pair: -abs(pair[1]))
        ]

    def line_hop(hop, size, src_of, dst, sems, peer_of, me):
        return [
            start(src_of((me + k) % size), dst, sems[0].at[hop, k - 1], sems[1].at[hop, k - 1], peer_of(k))
            for k in far_first(size)
        ]

    def landed(copies):
        for copy in copies:
            copy.wait_recv()

    loads[0].wait()
    loads[1].wait()
    sent_ids = [[lists[0, h, i] for h in range(halo_blocks)] for i in range(len(OFFSETS))]
    for b in range(nb):
        x_own[b] = x_ref[:, 128 * b : 128 * (b + 1)]
    for i in range(len(OFFSETS)):
        for h in range(halo_blocks):
            x_halo_out[i, h] = x_own[sent_ids[i][h]]

    pl.semaphore_wait(barrier, arrivals)

    halo1 = halo_hop(0, x_halo_out, lambda i: src1.at[pl.ds(nb + halo_blocks * i, halo_blocks)], 1)
    x_all = feat_hop(0, lambda g: x_own, r1.at[:, f, 0])

    src1[pl.ds(0, nb)] = x_own[...]
    src1[total] = jnp.zeros((cols1, 128), BF16)
    src2[total] = jnp.zeros((cols2, 128), BF16)
    r1[:, f, 0] = x_own[...]
    for load in loads[2:5]:
        load.wait()
    targets = [
        [jnp.where(j < counts[b], ids[j, b], total) for j in range(ns)] for b in range(nb)
    ]
    for b in range(nb):
        ones = jnp.concatenate(
            [
                jnp.full((16, 128), jnp.where(targets[b][j] < total, 1.0, 0.0), F32)
                for j in range(ns)
            ],
            1,
        ).astype(BF16)
        deg = sum(mm(ones[:, 128 * j : 128 * (j + 1)], adj[b, j], NT) for j in range(ns))
        rdeg[b] = 1.0 / deg[0:8]
    for load in loads[5:]:
        load.wait()
    for g in range(nf):
        w1i[g, 0:cols1] = w1s[cols1 * g : cols1 * (g + 1)]
        w1i[g, cols1:] = w1n[cols1 * g : cols1 * (g + 1)]
    w1t[...] = w1i[...].reshape(2 * nf * cols1, hid).T.reshape(w1t.shape)
    w2t[:, 0:hid] = w2s[...].T
    w2t[:, hid:] = w2n[...].T
    up_t[...] = up[...].T

    def aggregate(src, out):
        for b in range(nb):
            total_b = sum(mm(src[targets[b][j]], adj[b, j], NT) for j in range(ns))
            out[b] = (total_b * rdeg[b][0:1]).astype(BF16)

    def dense(out, first):
        def body(b, carry):
            rows = pl.ds(pl.multiple_of(b * 128, 128), 128)
            for n in range(nb):
                tile = jnp.zeros((8, 16, 128), BF16)
                for j in range(ns):
                    here = jnp.logical_and(j < counts[b], ids[j, b] == first + n)
                    mask = jnp.full((16, 128), jnp.where(here, 1.0, 0.0), F32).astype(BF16)
                    tile = tile + adj[b, j].reshape(8, 16, 128) * mask[None]
                out[rows, 128 * n : 128 * (n + 1)] = tile.reshape(128, 128)
            return carry

        lax.fori_loop(0, nb, body, 0)

    def all_blocks(u, lo, c):
        return jnp.concatenate([u[b][lo : lo + c] for b in range(nb)], 1)

    def halo_sums(u, out, c):
        sums = mm(u, to_halo[...]).astype(BF16)
        for n in range(len(OFFSETS) * halo_blocks):
            out[n // halo_blocks, n % halo_blocks] = sums[:, 128 * n : 128 * (n + 1)]

    def with_returned(back, n, c):
        acc = part[0:c, 128 * n : 128 * (n + 1)]
        for i in range(len(OFFSETS)):
            for h in range(halo_blocks):
                here = jnp.where(sent_ids[i][h] == n, 1.0, 0.0)
                acc = acc + here * back[i, h].astype(F32)
        return acc

    landed(halo1)
    aggregate(src1, agg1_col)
    agg1_all = feat_hop(1, lambda g: agg1_col, r1.at[:, f, 1])
    r1[:, f, 1] = agg1_col[...]
    dense(to_halo, nb)
    landed(x_all)
    landed(agg1_all)
    blocks1 = [r1[b].reshape(2 * nf * cols1, 128) for b in range(nb)]
    first_cols = mm(w1t[f], jnp.concatenate(blocks1, 1))
    gate = jax.nn.sigmoid(first_cols)
    hidden_cols = (first_cols * gate).astype(BF16)
    for b in range(nb):
        h_own[b] = hidden_cols[:, 128 * b : 128 * (b + 1)]
    for i in range(len(OFFSETS)):
        for h in range(halo_blocks):
            h_halo_out[i, h] = h_own[sent_ids[i][h]]
    halo2 = halo_hop(1, h_halo_out, lambda i: src2.at[pl.ds(nb + halo_blocks * i, halo_blocks)], 1)
    slopes = slope_of(first_cols, gate)
    for b in range(nb):
        slope1_col[b] = slopes[:, 128 * b : 128 * (b + 1)]
    for i in range(len(OFFSETS)):
        for h in range(halo_blocks):
            slope_halo_out[i, h] = slope1_col[sent_ids[i][h]].astype(BF16)
            r1_halo_out[i, h] = r1[sent_ids[i][h]]
    slope_halo = halo_hop(4, slope_halo_out, lambda i: slope_halo_in.at[i], 1)
    r1_halo = halo_hop(5, r1_halo_out, lambda i: r1_halo_in.at[i], 1)
    first_pre = mm(w1t[...].reshape(hid, 2 * nf * cols1), r1[f].reshape(2 * nf * cols1, 128))
    gate = jax.nn.sigmoid(first_pre)
    row2[0:nf] = (first_pre * gate).astype(BF16).reshape(nf, cols2, 128)
    slope1[...] = slope_of(first_pre, gate)

    src2[pl.ds(0, nb)] = h_own[...]
    landed(halo2)
    aggregate(src2, agg2_col)
    agg2_rows = feat_hop(2, lambda g: agg2_col.at[g], row2.at[nf + f])
    row2[nf + f] = agg2_col[f]
    dense(to_own, 0)
    landed(agg2_rows)
    rows2 = row2[...].reshape(2 * hid, 128)
    second_pre = mm(w2t[...], rows2)
    gate = jax.nn.sigmoid(second_pre)
    delta_two = (up_t[...].astype(F32) * slope_of(second_pre, gate)).astype(BF16)
    d2[...] = delta_two
    own_rdeg = rdeg[f][0:1]
    u2_row[:, 0:cols2] = (mm(w2n[...], delta_two) * own_rdeg).astype(BF16).reshape(nf, cols2, 128)
    self_two = mm(w2s[...], delta_two).astype(BF16)
    self2[...] = self_two
    u2_row[:, cols2:] = self_two.reshape(nf, cols2, 128)
    u2_cols = feat_hop(3, lambda g: u2_row.at[g], u2_col.at[f])
    u2_col[f] = u2_row[f]

    grad2 = mm(rows2, delta_two, NT).astype(BF16)
    g2_out[:, 0:cols2] = grad2[0:hid].reshape(nf, cols2, hid)
    g2_out[:, cols2:] = grad2[hid:].reshape(nf, cols2, hid)
    g2_feat = feat_hop(4, lambda g: g2_out.at[g], g2_in.at[f])
    g2_in[f] = g2_out[f]
    act_o[...] = (second_pre * gate).T.astype(BF16)
    stores[0].start()

    landed(u2_cols)
    u2_all = all_blocks(u2_col, 0, cols2)
    halo_sums(u2_all, back2_out, cols2)
    back2 = halo_hop(2, back2_out, lambda i: back2_in.at[i], -1)
    part[...] = mm(u2_all, to_own[...])

    landed(slope_halo)
    landed(r1_halo)
    grad1 = jnp.zeros((cols2, 2 * nf * cols1), F32)
    for n in range(nb):
        hidden_grad = u2_col[n][cols2:].astype(F32) + part[:, 128 * n : 128 * (n + 1)]
        delta_cols = (hidden_grad * slope1_col[n]).astype(BF16)
        grad1 = grad1 + mm(delta_cols, r1[n].reshape(2 * nf * cols1, 128), NT)
    for i in range(len(OFFSETS)):
        for h in range(halo_blocks):
            delta_cols = (back2_out[i, h].astype(F32) * slope_halo_in[i, h].astype(F32)).astype(BF16)
            grad1 = grad1 + mm(delta_cols, r1_halo_in[i, h].reshape(2 * nf * cols1, 128), NT)
    group = lax.broadcasted_iota(jnp.int32, (8, 128), 1) // (2 * cols1)
    for g in range(nf):
        lane = 2 * cols1 * g
        wide = grad1[:, lane // 128 * 128 : lane // 128 * 128 + 128]
        packed = jnp.zeros((8, 128), F32)
        for q in range(128 // (2 * cols1)):
            shift = (2 * cols1 * q - lane) % 128
            piece = wide[8 * q : 8 * (q + 1)]
            packed = jnp.where(group == q, pltpu.roll(piece, shift, 1) if shift else piece, packed)
        g1y_out[g] = packed
    y_sems, z_sems = (y_send, y_recv), (z_send, z_recv)
    g1_y = line_hop(1, ny, lambda g: g1y_out.at[g], g1y_in.at[y], y_sems, y_peer, y)
    g1y_in[y] = g1y_out[y]

    landed(g2_feat)
    g2_sum = g2_in[0].astype(F32)
    for k in range(1, nf):
        g2_sum = g2_sum + g2_in[k].astype(F32)
    g2y_out[...] = g2_sum.reshape(g2y_out.shape)
    g2_y = line_hop(0, ny, lambda g: g2y_out.at[g], g2y_in.at[y], y_sems, y_peer, y)
    g2y_in[y] = g2y_out[y]

    landed(back2)
    for n in range(nb):
        sp2_col[n] = with_returned(back2_in, n, cols2).astype(BF16)
    sp2_rows = feat_hop(5, lambda g: sp2_col.at[g], sp2_row.at[f])
    sp2_row[f] = sp2_col[f]

    landed(g1_y)
    g1z_out[...] = jnp.sum(g1y_in[...], 0)
    g1_z = line_hop(1, nz, lambda g: g1z_out, g1z_in.at[z], z_sems, z_peer, z)
    g1z_in[z] = g1z_out[...]

    landed(g2_y)
    g2_chunk = jnp.sum(g2y_in[...], 0)
    for a in range(hid // 128):
        g2z_out[8 * a : 8 * (a + 1)] = g2_chunk[:, 128 * a : 128 * (a + 1)].astype(BF16)
    g2_z = line_hop(0, nz, lambda g: g2z_out, g2z_in.at[z], z_sems, z_peer, z)
    g2z_in[z] = g2z_out[...]

    landed(sp2_rows)
    hidden_grad = (
        self2[...].astype(F32) + sp2_row[...].reshape(hid, 128).astype(F32)
    ).astype(BF16)
    delta_one = (hidden_grad.astype(F32) * slope1[...]).astype(BF16)
    back = mm(w1i[...].reshape(2 * nf * cols1, hid), delta_one).reshape(nf, 2 * cols1, 128)
    u1_row[:, 0:cols1] = back[:, 0:cols1].astype(BF16)
    u1_row[:, cols1:] = (back[:, cols1:] * own_rdeg).astype(BF16)
    u1_cols = feat_hop(6, lambda g: u1_row.at[g], u1_col.at[f])
    u1_col[f] = u1_row[f]

    drain()
    landed(u1_cols)
    u1_all = all_blocks(u1_col, cols1, cols1)
    halo_sums(u1_all, back1_out, cols1)
    back1 = halo_hop(3, back1_out, lambda i: back1_in.at[i], -1)
    part[0:cols1] = mm(u1_all, to_own[...])

    landed(g1_z)
    g1_own[...] = jnp.sum(g1z_in[...], 0) * scale
    cross = [
        pltpu.make_async_remote_copy(
            src_ref=g1_own,
            dst_ref=g1_all.at[f],
            send_sem=cross_send.at[k],
            recv_sem=cross_recv.at[f],
            device_id=(((y + k) % ny) * nz + z, y),
            device_id_type=MESH,
        )
        for k in range(ny)
    ]
    for k in far_first(ny):
        cross[k].start()

    @pl.when(f != y)
    def _():
        cross[0].start()

    @pl.when(f == y)
    def _():
        g1_all[f] = g1_own[...]

    landed(g2_z)
    g2_final = jnp.sum(g2z_in[...].astype(F32), 0) * scale
    for a in range(hid // 128):
        g2_all[y, :, 128 * a : 128 * (a + 1)] = g2_final[8 * a : 8 * (a + 1)]
    g2_back = line_hop(2, ny, lambda g: g2_all.at[y], g2_all.at[y], y_sems, y_peer, y)

    landed(back1)
    for n in range(nb):
        fg_o[:, 128 * n : 128 * (n + 1)] = (
            u1_col[n][0:cols1].astype(F32) + with_returned(back1_in, n, cols1)
        ).astype(BF16)
    stores[1].start()

    landed(g2_back)
    grads = g2_all[...].reshape(2 * cols2, hid)
    g2s_o[...] = grads[0:cols2]
    g2n_o[...] = grads[cols2:]
    stores[4].start()
    stores[5].start()

    drain()
    for s in range(nf):

        @pl.when(jnp.logical_or(f != y, f != s))
        def _():
            pltpu.make_async_remote_copy(
                src_ref=g1_own,
                dst_ref=g1_all.at[s],
                send_sem=cross_send.at[0],
                recv_sem=cross_recv.at[s],
                device_id=(f * nz + z, s),
                device_id_type=MESH,
            ).wait_recv()

    tiles = []
    for s in range(nf):
        tile = g1_all[s]
        for q in range(128 // (2 * cols1)):
            tiles.append(pltpu.roll(tile, 128 - 2 * cols1 * q, 1) if q else tile)
    grad1_rows = jnp.concatenate(tiles, 0).T
    g1s_o[...] = grad1_rows[0:cols1]
    g1n_o[...] = grad1_rows[cols1 : 2 * cols1]
    stores[2].start()
    stores[3].start()

    for k in range(1, ny):
        cross[k].wait_send()

    @pl.when(f != y)
    def _():
        cross[0].wait_send()

    for copy in stores:
        copy.wait()


def store(count, *refs):
    ins, outs, held = refs[:count], refs[count : 2 * count], refs[2 * count : 3 * count]
    sems = refs[-1]
    fetch = [pltpu.make_async_copy(ins[i], held[i], sems.at[0, i]) for i in range(count)]
    write = [pltpu.make_async_copy(held[i], outs[i], sems.at[1, i]) for i in range(count)]
    for copy in fetch:
        copy.start()
    for first, second in zip(fetch, write):
        first.wait()
        second.start()
    for copy in write:
        copy.wait()


def on_device(
    features,
    adjacency,
    source_ids,
    counts,
    send_lists,
    first_self,
    first_neighbour,
    second_self,
    second_neighbour,
    upstream,
):
    nodes, nf = lax.axis_size("nodes"), lax.axis_size("feat")
    ny = 8
    nz = nodes // ny
    nb, ns, bs = adjacency.shape[0], adjacency.shape[1], adjacency.shape[2]
    hs = send_lists.shape[2]
    total = nb + len(OFFSETS) * hs
    c1 = features.shape[1]
    hid = upstream.shape[1]
    c2 = hid // nf
    noff = len(OFFSETS)
    scale = 1.0 / math.sqrt(nb * bs * nodes)
    hbm = pl.BlockSpec(memory_space=pltpu.HBM)
    scratch = [
        ((bs, hid), BF16),
        ((c1, nb * bs), BF16),
        ((c1, hid), F32),
        ((c1, hid), F32),
        ((c2, hid), F32),
        ((c2, hid), F32),
        ((c1, nb * bs), BF16),
        (adjacency.shape, BF16),
        (first_self.shape, BF16),
        (first_neighbour.shape, BF16),
        (second_self.shape, BF16),
        (second_neighbour.shape, BF16),
        (upstream.shape, BF16),
        ((nf, 2 * c1, hid), BF16),
        ((nf, c2, 2 * nf * c1), BF16),
        ((hid, 2 * hid), BF16),
        ((hid, bs), BF16),
        ((nb, 8, bs), F32),
        ((nb, c1, bs), BF16),
        ((noff, hs, c1, bs), BF16),
        ((total + 1, c1, bs), BF16),
        ((nb, c1, bs), BF16),
        ((nb, nf, 2, c1, bs), BF16),
        ((hid, bs), F32),
        ((nb, c2, bs), F32),
        ((noff, hs, c2, bs), BF16),
        ((noff, hs, c2, bs), BF16),
        ((noff, hs, nf, 2, c1, bs), BF16),
        ((noff, hs, nf, 2, c1, bs), BF16),
        ((2 * nf, c2, bs), BF16),
        ((nb, c2, bs), BF16),
        ((noff, hs, c2, bs), BF16),
        ((total + 1, c2, bs), BF16),
        ((nb, c2, bs), BF16),
        ((hid, bs), BF16),
        ((hid, bs), BF16),
        ((nf, 2 * c2, bs), BF16),
        ((nb, 2 * c2, bs), BF16),
        ((nb * bs, noff * hs * bs), BF16),
        ((nb * bs, nb * bs), BF16),
        ((c2, nb * bs), F32),
        ((noff, hs, c2, bs), BF16),
        ((noff, hs, c2, bs), BF16),
        ((nb, c2, bs), BF16),
        ((nf, c2, bs), BF16),
        ((nf, 2 * c1, bs), BF16),
        ((nb, 2 * c1, bs), BF16),
        ((noff, hs, c1, bs), BF16),
        ((noff, hs, c1, bs), BF16),
        ((nf, 2 * c2, hid), BF16),
        ((nf, 2 * c2, hid), BF16),
        ((ny, 2 * c2 // ny, hid), F32),
        ((ny, 2 * c2 // ny, hid), F32),
        ((16, 128), BF16),
        ((nz, 16, 128), BF16),
        ((ny, 2 * c2 // ny, hid), F32),
        ((ny, 8, 128), F32),
        ((ny, 8, 128), F32),
        ((8, 128), F32),
        ((nz, 8, 128), F32),
        ((8, 128), F32),
        ((nf, 8, 128), F32),
    ]
    dma = pltpu.SemaphoreType.DMA
    outs = pl.pallas_call(
        functools.partial(kernel, (nodes, ny, nz, nf, nb, ns), scale),
        out_shape=(
            jax.ShapeDtypeStruct((bs, hid), BF16),
            jax.ShapeDtypeStruct((c1, nb * bs), BF16),
            jax.ShapeDtypeStruct((c1, hid), F32),
            jax.ShapeDtypeStruct((c1, hid), F32),
            jax.ShapeDtypeStruct((c2, hid), F32),
            jax.ShapeDtypeStruct((c2, hid), F32),
        ),
        in_specs=[hbm] * 10,
        out_specs=(hbm,) * 6,
        scratch_shapes=[pltpu.VMEM(shape, kind) for shape, kind in scratch[:6]]
        + [
            pltpu.SMEM((ns, nb), jnp.int32),
            pltpu.SMEM((nb,), jnp.int32),
            pltpu.SMEM((1, hs, noff), jnp.int32),
        ]
        + [pltpu.VMEM(shape, kind) for shape, kind in scratch[6:]]
        + [
            dma((7, nf - 1)),
            dma((7, nf - 1)),
            dma((6, noff)),
            dma((6, noff)),
            dma((3, ny - 1)),
            dma((3, ny - 1)),
            dma((2, nz - 1)),
            dma((2, nz - 1)),
            dma((ny,)),
            dma((nf,)),
            dma((10,)),
            dma((6,)),
        ],
        compiler_params=pltpu.CompilerParams(
            collective_id=0, has_side_effects=True, vmem_limit_bytes=60 * 1024 * 1024
        ),
    )(
        source_ids.T,
        counts,
        send_lists.transpose(0, 2, 1),
        features.T,
        adjacency,
        first_self,
        first_neighbour,
        second_self,
        second_neighbour,
        upstream,
    )
    outs = pl.pallas_call(
        functools.partial(store, len(outs)),
        out_shape=tuple(jax.ShapeDtypeStruct(o.shape, o.dtype) for o in outs),
        in_specs=[hbm] * len(outs),
        out_specs=(hbm,) * len(outs),
        scratch_shapes=[pltpu.VMEM(o.shape, o.dtype) for o in outs] + [dma((2, len(outs)))],
        compiler_params=pltpu.CompilerParams(vmem_limit_bytes=60 * 1024 * 1024),
    )(*outs)
    return (outs[0], outs[1].T) + tuple(outs[2:])


def solution(mesh):
    return jax.shard_map(
        on_device,
        mesh=mesh,
        in_specs=(
            P("nodes", "feat"),
            P("nodes", None, None, None),
            P("nodes", None),
            P("nodes"),
            P("nodes", None, None),
            P(),
            P(),
            P(),
            P(),
            P(("nodes", "feat"), None),
        ),
        out_specs=(
            P(("nodes", "feat"), None),
            P("nodes", "feat"),
            P("feat", None),
            P("feat", None),
            P("feat", None),
            P("feat", None),
        ),
        check_vma=False,
    )
```

```python
import functools
import math

import jax
import jax.numpy as jnp
from jax import lax
from jax.experimental import pallas as pl
from jax.experimental.pallas import tpu as pltpu
from jax.sharding import PartitionSpec as P

OFFSETS = (1, -1, 2, -2)
MESH = pl.DeviceIdType.MESH
F32, BF16 = jnp.float32, jnp.bfloat16
NN = (((1,), (0,)), ((), ()))
NT = (((1,), (1,)), ((), ()))


def mm(lhs, rhs, dims=NN):
    return lax.dot_general(lhs, rhs, dims, preferred_element_type=F32)


def slope_of(values, gate):
    return gate * (1.0 + values * (1.0 - gate))


def kernel(
    sizes,
    scale,
    ids_in,
    counts_in,
    lists_in,
    x_in,
    adj_in,
    w1s_in,
    w1n_in,
    w2s_in,
    w2n_in,
    up_in,
    act_out,
    fg_out,
    g1s_out,
    g1n_out,
    g2s_out,
    g2n_out,
    act_o,
    fg_o,
    g1s_o,
    g1n_o,
    g2s_o,
    g2n_o,
    ids,
    counts,
    lists,
    x_ref,
    adj,
    w1s,
    w1n,
    w2s,
    w2n,
    up,
    w1i,
    w1t,
    w2t,
    up_t,
    rdeg,
    x_own,
    x_halo_out,
    src1,
    agg1_col,
    r1,
    slope1,
    slope1_col,
    slope_halo_out,
    slope_halo_in,
    r1_halo_out,
    r1_halo_in,
    row2,
    h_own,
    h_halo_out,
    src2,
    agg2_col,
    d2,
    self2,
    u2_row,
    u2_col,
    to_halo,
    to_own,
    part,
    back2_out,
    back2_in,
    sp2_col,
    sp2_row,
    u1_row,
    u1_col,
    back1_out,
    back1_in,
    g2_out,
    g2_in,
    g2y_out,
    g2y_in,
    g2z_out,
    g2z_in,
    g2_all,
    g1y_out,
    g1y_in,
    g1z_out,
    g1z_in,
    g1_own,
    g1_all,
    feat_send,
    feat_recv,
    halo_send,
    halo_recv,
    y_send,
    y_recv,
    z_send,
    z_recv,
    cross_send,
    cross_recv,
    load_sems,
    store_sems,
):
    nodes, ny, nz, nf, nb, ns = sizes
    p = lax.axis_index("nodes")
    f = lax.axis_index("feat")
    y, z = p // nz, p % nz
    cols1, cols2 = x_own.shape[1], h_own.shape[1]
    hid = d2.shape[0]
    halo_blocks = x_halo_out.shape[1]
    total = nb + len(OFFSETS) * halo_blocks

    def feat_peer(k):
        return (p, (f + k) % nf)

    def node_peer(offset):
        return ((p + nodes + offset) % nodes, f)

    def y_peer(k):
        return (((y + k) % ny) * nz + z, f)

    def z_peer(k):
        return (y * nz + (z + k) % nz, f)

    def far_first(size):
        return sorted(range(1, size), key=lambda k: -min(k, size - k))

    loads = [
        pltpu.make_async_copy(src, dst, load_sems.at[i])
        for i, (src, dst) in enumerate(
            (
                (x_in, x_ref),
                (lists_in, lists),
                (ids_in, ids),
                (counts_in, counts),
                (adj_in, adj),
                (w1s_in, w1s),
                (w1n_in, w1n),
                (w2s_in, w2s),
                (w2n_in, w2n),
                (up_in, up),
            )
        )
    ]
    for load in loads:
        load.start()
    stores = [
        pltpu.make_async_copy(src, dst, store_sems.at[i])
        for i, (src, dst) in enumerate(
            (
                (act_o, act_out),
                (fg_o, fg_out),
                (g1s_o, g1s_out),
                (g1n_o, g1n_out),
                (g2s_o, g2s_out),
                (g2n_o, g2n_out),
            )
        )
    ]

    barrier = pltpu.get_barrier_semaphore()
    peers = (
        [node_peer(o) for o in OFFSETS]
        + [feat_peer(k) for k in range(1, nf)]
        + [y_peer(k) for k in range(1, ny)]
        + [z_peer(k) for k in range(1, nz)]
    )
    for peer in peers:
        pl.semaphore_signal(barrier, inc=1, device_id=peer, device_id_type=MESH)
    for s in range(nf):

        @pl.when(jnp.logical_or(f != y, f != s))
        def _():
            pl.semaphore_signal(barrier, inc=1, device_id=(f * nz + z, s), device_id_type=MESH)

    arrivals = len(peers) + ny - jnp.where(f == y, 1, 0)

    sent = []

    def drain():
        while sent:
            sent.pop(0).wait_send()

    def start(src, dst, ssem, rsem, peer):
        copy = pltpu.make_async_remote_copy(
            src_ref=src, dst_ref=dst, send_sem=ssem, recv_sem=rsem, device_id=peer, device_id_type=MESH
        )
        copy.start()
        sent.append(copy)
        return copy

    def feat_hop(hop, src_of, dst):
        copies = []
        for k in far_first(nf):
            g = (f + k) % nf
            copies.append(
                start(src_of(g), dst, feat_send.at[hop, k - 1], feat_recv.at[hop, k - 1], feat_peer(k))
            )
        return copies

    def halo_hop(hop, src, dst_of, sign):
        return [
            start(src.at[i], dst_of(i), halo_send.at[hop, i], halo_recv.at[hop, i], node_peer(sign * o))
            for i, o in sorted(enumerate(OFFSETS), key=lambda pair: -abs(pair[1]))
        ]

    def line_hop(hop, size, src_of, dst, sems, peer_of, me):
        return [
            start(src_of((me + k) % size), dst, sems[0].at[hop, k - 1], sems[1].at[hop, k - 1], peer_of(k))
            for k in far_first(size)
        ]

    def landed(copies):
        for copy in copies:
            copy.wait_recv()

    loads[0].wait()
    loads[1].wait()
    sent_ids = [[lists[0, h, i] for h in range(halo_blocks)] for i in range(len(OFFSETS))]
    for b in range(nb):
        x_own[b] = x_ref[:, 128 * b : 128 * (b + 1)]
    for i in range(len(OFFSETS)):
        for h in range(halo_blocks):
            x_halo_out[i, h] = x_own[sent_ids[i][h]]

    pl.semaphore_wait(barrier, arrivals)

    halo1 = halo_hop(0, x_halo_out, lambda i: src1.at[pl.ds(nb + halo_blocks * i, halo_blocks)], 1)
    x_all = feat_hop(0, lambda g: x_own, r1.at[:, f, 0])

    src1[pl.ds(0, nb)] = x_own[...]
    src1[total] = jnp.zeros((cols1, 128), BF16)
    src2[total] = jnp.zeros((cols2, 128), BF16)
    r1[:, f, 0] = x_own[...]
    for load in loads[2:5]:
        load.wait()
    targets = [
        [jnp.where(j < counts[b], ids[j, b], total) for j in range(ns)] for b in range(nb)
    ]
    for b in range(nb):
        ones = jnp.concatenate(
            [
                jnp.full((16, 128), jnp.where(targets[b][j] < total, 1.0, 0.0), F32)
                for j in range(ns)
            ],
            1,
        ).astype(BF16)
        deg = sum(mm(ones[:, 128 * j : 128 * (j + 1)], adj[b, j], NT) for j in range(ns))
        rdeg[b] = 1.0 / deg[0:8]
    for load in loads[5:]:
        load.wait()
    for g in range(nf):
        w1i[g, 0:cols1] = w1s[cols1 * g : cols1 * (g + 1)]
        w1i[g, cols1:] = w1n[cols1 * g : cols1 * (g + 1)]
    w1t[...] = w1i[...].reshape(2 * nf * cols1, hid).T.reshape(w1t.shape)

    def aggregate(src, out):
        for b in range(nb):
            total_b = sum(mm(src[targets[b][j]], adj[b, j], NT) for j in range(ns))
            out[b] = (total_b * rdeg[b][0:1]).astype(BF16)

    def dense(out, first, low, high):
        def body(b, carry):
            rows = pl.ds(pl.multiple_of(b * 128, 128), 128)
            for n in range(nb):
                tile = jnp.zeros((8, 16, 128), BF16)
                for j in range(ns):
                    here = jnp.logical_and(j < counts[b], ids[j, b] == first + n)
                    mask = jnp.full((16, 128), jnp.where(here, 1.0, 0.0), F32).astype(BF16)
                    tile = tile + adj[b, j].reshape(8, 16, 128) * mask[None]
                out[rows, 128 * n : 128 * (n + 1)] = tile.reshape(128, 128)
            return carry

        lax.fori_loop(low, high, body, 0)

    def all_blocks(u, lo, c):
        return jnp.concatenate([u[b][lo : lo + c] for b in range(nb)], 1)

    def halo_sums(u, out, c):
        sums = mm(u, to_halo[...]).astype(BF16)
        for n in range(len(OFFSETS) * halo_blocks):
            out[n // halo_blocks, n % halo_blocks] = sums[:, 128 * n : 128 * (n + 1)]

    def with_returned(back, n, c):
        acc = part[0:c, 128 * n : 128 * (n + 1)]
        for i in range(len(OFFSETS)):
            for h in range(halo_blocks):
                here = jnp.where(sent_ids[i][h] == n, 1.0, 0.0)
                acc = acc + here * back[i, h].astype(F32)
        return acc

    landed(halo1)
    aggregate(src1, agg1_col)
    agg1_all = feat_hop(1, lambda g: agg1_col, r1.at[:, f, 1])
    r1[:, f, 1] = agg1_col[...]
    dense(to_halo, nb, 0, nb // 2)
    w2t[:, 0:hid] = w2s[...].T
    w2t[:, hid:] = w2n[...].T
    up_t[...] = up[...].T
    landed(x_all)
    landed(agg1_all)
    blocks1 = [r1[b].reshape(2 * nf * cols1, 128) for b in range(nb)]
    first_cols = mm(w1t[f], jnp.concatenate(blocks1, 1))
    gate = jax.nn.sigmoid(first_cols)
    hidden_cols = (first_cols * gate).astype(BF16)
    for b in range(nb):
        h_own[b] = hidden_cols[:, 128 * b : 128 * (b + 1)]
    for i in range(len(OFFSETS)):
        for h in range(halo_blocks):
            h_halo_out[i, h] = h_own[sent_ids[i][h]]
    halo2 = halo_hop(1, h_halo_out, lambda i: src2.at[pl.ds(nb + halo_blocks * i, halo_blocks)], 1)
    slopes = slope_of(first_cols, gate)
    for b in range(nb):
        slope1_col[b] = slopes[:, 128 * b : 128 * (b + 1)]
    for i in range(len(OFFSETS)):
        for h in range(halo_blocks):
            slope_halo_out[i, h] = slope1_col[sent_ids[i][h]].astype(BF16)
            r1_halo_out[i, h] = r1[sent_ids[i][h]]
    slope_halo = halo_hop(4, slope_halo_out, lambda i: slope_halo_in.at[i], 1)
    r1_halo = halo_hop(5, r1_halo_out, lambda i: r1_halo_in.at[i], 1)
    first_pre = mm(w1t[...].reshape(hid, 2 * nf * cols1), r1[f].reshape(2 * nf * cols1, 128))
    gate = jax.nn.sigmoid(first_pre)
    row2[0:nf] = (first_pre * gate).astype(BF16).reshape(nf, cols2, 128)
    slope1[...] = slope_of(first_pre, gate)
    dense(to_halo, nb, nb // 2, nb)

    src2[pl.ds(0, nb)] = h_own[...]
    landed(halo2)
    aggregate(src2, agg2_col)
    agg2_rows = feat_hop(2, lambda g: agg2_col.at[g], row2.at[nf + f])
    row2[nf + f] = agg2_col[f]
    dense(to_own, 0, 0, nb // 2)
    landed(agg2_rows)
    rows2 = row2[...].reshape(2 * hid, 128)
    second_pre = mm(w2t[...], rows2)
    gate = jax.nn.sigmoid(second_pre)
    delta_two = (up_t[...].astype(F32) * slope_of(second_pre, gate)).astype(BF16)
    d2[...] = delta_two
    own_rdeg = rdeg[f][0:1]
    u2_row[:, 0:cols2] = (mm(w2n[...], delta_two) * own_rdeg).astype(BF16).reshape(nf, cols2, 128)
    self_two = mm(w2s[...], delta_two).astype(BF16)
    self2[...] = self_two
    u2_row[:, cols2:] = self_two.reshape(nf, cols2, 128)
    u2_cols = feat_hop(3, lambda g: u2_row.at[g], u2_col.at[f])
    u2_col[f] = u2_row[f]

    grad2 = mm(rows2, delta_two, NT).astype(BF16)
    g2_out[:, 0:cols2] = grad2[0:hid].reshape(nf, cols2, hid)
    g2_out[:, cols2:] = grad2[hid:].reshape(nf, cols2, hid)
    g2_feat = feat_hop(4, lambda g: g2_out.at[g], g2_in.at[f])
    g2_in[f] = g2_out[f]
    act_o[...] = (second_pre * gate).T.astype(BF16)
    stores[0].start()
    dense(to_own, 0, nb // 2, nb)

    landed(u2_cols)
    u2_all = all_blocks(u2_col, 0, cols2)
    halo_sums(u2_all, back2_out, cols2)
    back2 = halo_hop(2, back2_out, lambda i: back2_in.at[i], -1)
    part[...] = mm(u2_all, to_own[...])

    landed(slope_halo)
    landed(r1_halo)
    deltas, rows = [], []
    for n in range(nb):
        hidden_grad = u2_col[n][cols2:].astype(F32) + part[:, 128 * n : 128 * (n + 1)]
        deltas.append((hidden_grad * slope1_col[n]).astype(BF16))
        rows.append(r1[n].reshape(2 * nf * cols1, 128))
    for i in range(len(OFFSETS)):
        for h in range(halo_blocks):
            returned = back2_out[i, h].astype(F32) * slope_halo_in[i, h].astype(F32)
            deltas.append(returned.astype(BF16))
            rows.append(r1_halo_in[i, h].reshape(2 * nf * cols1, 128))
    copies = 128 // cols2
    grad1 = mm(
        jnp.concatenate(rows, 1), jnp.concatenate([jnp.concatenate(deltas, 1)] * copies, 0), NT
    )
    group = lax.broadcasted_iota(jnp.int32, (8, 128), 1) // cols2
    for g in range(nf):
        packed = jnp.zeros((8, 128), F32)
        for q in range(copies):
            row = 2 * cols1 * g + 8 * q
            packed = jnp.where(group == q, grad1[row : row + 8], packed)
        g1y_out[g] = packed
    y_sems, z_sems = (y_send, y_recv), (z_send, z_recv)
    g1_y = line_hop(1, ny, lambda g: g1y_out.at[g], g1y_in.at[y], y_sems, y_peer, y)
    g1y_in[y] = g1y_out[y]

    landed(g2_feat)
    g2_sum = g2_in[0].astype(F32)
    for k in range(1, nf):
        g2_sum = g2_sum + g2_in[k].astype(F32)
    for g in range(ny):
        for a in range(hid // 128):
            chunk = g2_sum[8 * g : 8 * (g + 1), 128 * a : 128 * (a + 1)]
            g2y_out[g, 8 * a : 8 * (a + 1)] = chunk.astype(BF16)
    g2_y = line_hop(0, ny, lambda g: g2y_out.at[g], g2y_in.at[y], y_sems, y_peer, y)
    g2y_in[y] = g2y_out[y]

    landed(back2)
    for n in range(nb):
        sp2_col[n] = with_returned(back2_in, n, cols2).astype(BF16)
    sp2_rows = feat_hop(5, lambda g: sp2_col.at[g], sp2_row.at[f])
    sp2_row[f] = sp2_col[f]

    landed(g1_y)
    g1z_out[...] = jnp.sum(g1y_in[...], 0)
    g1_z = line_hop(1, nz, lambda g: g1z_out, g1z_in.at[z], z_sems, z_peer, z)
    g1z_in[z] = g1z_out[...]

    landed(g2_y)
    g2z_out[...] = jnp.sum(g2y_in[...].astype(F32), 0).astype(BF16)
    g2_z = line_hop(0, nz, lambda g: g2z_out, g2z_in.at[z], z_sems, z_peer, z)
    g2z_in[z] = g2z_out[...]

    landed(sp2_rows)
    hidden_grad = (
        self2[...].astype(F32) + sp2_row[...].reshape(hid, 128).astype(F32)
    ).astype(BF16)
    delta_one = (hidden_grad.astype(F32) * slope1[...]).astype(BF16)
    back = mm(w1i[...].reshape(2 * nf * cols1, hid), delta_one).reshape(nf, 2 * cols1, 128)
    u1_row[:, 0:cols1] = back[:, 0:cols1].astype(BF16)
    u1_row[:, cols1:] = (back[:, cols1:] * own_rdeg).astype(BF16)
    u1_cols = feat_hop(6, lambda g: u1_row.at[g], u1_col.at[f])
    u1_col[f] = u1_row[f]

    drain()
    landed(u1_cols)
    u1_all = all_blocks(u1_col, cols1, cols1)
    halo_sums(u1_all, back1_out, cols1)
    back1 = halo_hop(3, back1_out, lambda i: back1_in.at[i], -1)
    part[0:cols1] = mm(u1_all, to_own[...])

    landed(g1_z)
    g1_own[...] = jnp.sum(g1z_in[...], 0) * scale
    cross = [
        pltpu.make_async_remote_copy(
            src_ref=g1_own,
            dst_ref=g1_all.at[f],
            send_sem=cross_send.at[k],
            recv_sem=cross_recv.at[f],
            device_id=(((y + k) % ny) * nz + z, y),
            device_id_type=MESH,
        )
        for k in range(ny)
    ]
    for k in far_first(ny):
        cross[k].start()

    @pl.when(f != y)
    def _():
        cross[0].start()

    @pl.when(f == y)
    def _():
        g1_all[f] = g1_own[...]

    landed(g2_z)
    g2_final = jnp.sum(g2z_in[...].astype(F32), 0) * scale
    for a in range(hid // 128):
        g2_all[y, :, 128 * a : 128 * (a + 1)] = g2_final[8 * a : 8 * (a + 1)]
    g2_back = line_hop(2, ny, lambda g: g2_all.at[y], g2_all.at[y], y_sems, y_peer, y)

    landed(back1)
    for n in range(nb):
        fg_o[:, 128 * n : 128 * (n + 1)] = (
            u1_col[n][0:cols1].astype(F32) + with_returned(back1_in, n, cols1)
        ).astype(BF16)
    stores[1].start()

    landed(g2_back)
    grads = g2_all[...].reshape(2 * cols2, hid)
    g2s_o[...] = grads[0:cols2]
    g2n_o[...] = grads[cols2:]
    stores[4].start()
    stores[5].start()

    drain()
    for s in range(nf):

        @pl.when(jnp.logical_or(f != y, f != s))
        def _():
            pltpu.make_async_remote_copy(
                src_ref=g1_own,
                dst_ref=g1_all.at[s],
                send_sem=cross_send.at[0],
                recv_sem=cross_recv.at[s],
                device_id=(f * nz + z, s),
                device_id_type=MESH,
            ).wait_recv()

    for q in range(copies):
        out = g1s_o if 8 * q < cols1 else g1n_o
        row = 8 * q % cols1
        for a in range(hid // 128):
            wide = jnp.zeros((8, 128), F32)
            for t in range(copies):
                tile = g1_all[a * copies + t]
                shift = (t - q) * cols2 % 128
                wide = jnp.where(group == t, pltpu.roll(tile, shift, 1) if shift else tile, wide)
            out[row : row + 8, 128 * a : 128 * (a + 1)] = wide
    stores[2].start()
    stores[3].start()

    for k in range(1, ny):
        cross[k].wait_send()

    @pl.when(f != y)
    def _():
        cross[0].wait_send()

    for copy in stores:
        copy.wait()


def store(count, *refs):
    ins, outs, held = refs[:count], refs[count : 2 * count], refs[2 * count : 3 * count]
    sems = refs[-1]
    fetch = [pltpu.make_async_copy(ins[i], held[i], sems.at[0, i]) for i in range(count)]
    write = [pltpu.make_async_copy(held[i], outs[i], sems.at[1, i]) for i in range(count)]
    for copy in fetch:
        copy.start()
    for first, second in zip(fetch, write):
        first.wait()
        second.start()
    for copy in write:
        copy.wait()


def on_device(
    features,
    adjacency,
    source_ids,
    counts,
    send_lists,
    first_self,
    first_neighbour,
    second_self,
    second_neighbour,
    upstream,
):
    nodes, nf = lax.axis_size("nodes"), lax.axis_size("feat")
    ny = 8
    nz = nodes // ny
    nb, ns, bs = adjacency.shape[0], adjacency.shape[1], adjacency.shape[2]
    hs = send_lists.shape[2]
    total = nb + len(OFFSETS) * hs
    c1 = features.shape[1]
    hid = upstream.shape[1]
    c2 = hid // nf
    noff = len(OFFSETS)
    scale = 1.0 / math.sqrt(nb * bs * nodes)
    hbm = pl.BlockSpec(memory_space=pltpu.HBM)
    scratch = [
        ((bs, hid), BF16),
        ((c1, nb * bs), BF16),
        ((c1, hid), F32),
        ((c1, hid), F32),
        ((c2, hid), F32),
        ((c2, hid), F32),
        ((c1, nb * bs), BF16),
        (adjacency.shape, BF16),
        (first_self.shape, BF16),
        (first_neighbour.shape, BF16),
        (second_self.shape, BF16),
        (second_neighbour.shape, BF16),
        (upstream.shape, BF16),
        ((nf, 2 * c1, hid), BF16),
        ((nf, c2, 2 * nf * c1), BF16),
        ((hid, 2 * hid), BF16),
        ((hid, bs), BF16),
        ((nb, 8, bs), F32),
        ((nb, c1, bs), BF16),
        ((noff, hs, c1, bs), BF16),
        ((total + 1, c1, bs), BF16),
        ((nb, c1, bs), BF16),
        ((nb, nf, 2, c1, bs), BF16),
        ((hid, bs), F32),
        ((nb, c2, bs), F32),
        ((noff, hs, c2, bs), BF16),
        ((noff, hs, c2, bs), BF16),
        ((noff, hs, nf, 2, c1, bs), BF16),
        ((noff, hs, nf, 2, c1, bs), BF16),
        ((2 * nf, c2, bs), BF16),
        ((nb, c2, bs), BF16),
        ((noff, hs, c2, bs), BF16),
        ((total + 1, c2, bs), BF16),
        ((nb, c2, bs), BF16),
        ((hid, bs), BF16),
        ((hid, bs), BF16),
        ((nf, 2 * c2, bs), BF16),
        ((nb, 2 * c2, bs), BF16),
        ((nb * bs, noff * hs * bs), BF16),
        ((nb * bs, nb * bs), BF16),
        ((c2, nb * bs), F32),
        ((noff, hs, c2, bs), BF16),
        ((noff, hs, c2, bs), BF16),
        ((nb, c2, bs), BF16),
        ((nf, c2, bs), BF16),
        ((nf, 2 * c1, bs), BF16),
        ((nb, 2 * c1, bs), BF16),
        ((noff, hs, c1, bs), BF16),
        ((noff, hs, c1, bs), BF16),
        ((nf, 2 * c2, hid), BF16),
        ((nf, 2 * c2, hid), BF16),
        ((ny, 16, 128), BF16),
        ((ny, 16, 128), BF16),
        ((16, 128), BF16),
        ((nz, 16, 128), BF16),
        ((ny, 2 * c2 // ny, hid), F32),
        ((ny, 8, 128), F32),
        ((ny, 8, 128), F32),
        ((8, 128), F32),
        ((nz, 8, 128), F32),
        ((8, 128), F32),
        ((nf, 8, 128), F32),
    ]
    dma = pltpu.SemaphoreType.DMA
    outs = pl.pallas_call(
        functools.partial(kernel, (nodes, ny, nz, nf, nb, ns), scale),
        out_shape=(
            jax.ShapeDtypeStruct((bs, hid), BF16),
            jax.ShapeDtypeStruct((c1, nb * bs), BF16),
            jax.ShapeDtypeStruct((c1, hid), F32),
            jax.ShapeDtypeStruct((c1, hid), F32),
            jax.ShapeDtypeStruct((c2, hid), F32),
            jax.ShapeDtypeStruct((c2, hid), F32),
        ),
        in_specs=[hbm] * 10,
        out_specs=(hbm,) * 6,
        scratch_shapes=[pltpu.VMEM(shape, kind) for shape, kind in scratch[:6]]
        + [
            pltpu.SMEM((ns, nb), jnp.int32),
            pltpu.SMEM((nb,), jnp.int32),
            pltpu.SMEM((1, hs, noff), jnp.int32),
        ]
        + [pltpu.VMEM(shape, kind) for shape, kind in scratch[6:]]
        + [
            dma((7, nf - 1)),
            dma((7, nf - 1)),
            dma((6, noff)),
            dma((6, noff)),
            dma((3, ny - 1)),
            dma((3, ny - 1)),
            dma((2, nz - 1)),
            dma((2, nz - 1)),
            dma((ny,)),
            dma((nf,)),
            dma((10,)),
            dma((6,)),
        ],
        compiler_params=pltpu.CompilerParams(
            collective_id=0, has_side_effects=True, vmem_limit_bytes=60 * 1024 * 1024
        ),
    )(
        source_ids.T,
        counts,
        send_lists.transpose(0, 2, 1),
        features.T,
        adjacency,
        first_self,
        first_neighbour,
        second_self,
        second_neighbour,
        upstream,
    )
    outs = pl.pallas_call(
        functools.partial(store, len(outs)),
        out_shape=tuple(jax.ShapeDtypeStruct(o.shape, o.dtype) for o in outs),
        in_specs=[hbm] * len(outs),
        out_specs=(hbm,) * len(outs),
        scratch_shapes=[pltpu.VMEM(o.shape, o.dtype) for o in outs] + [dma((2, len(outs)))],
        compiler_params=pltpu.CompilerParams(vmem_limit_bytes=60 * 1024 * 1024),
    )(*outs)
    return (outs[0], outs[1].T) + tuple(outs[2:])


def solution(mesh):
    return jax.shard_map(
        on_device,
        mesh=mesh,
        in_specs=(
            P("nodes", "feat"),
            P("nodes", None, None, None),
            P("nodes", None),
            P("nodes"),
            P("nodes", None, None),
            P(),
            P(),
            P(),
            P(),
            P(("nodes", "feat"), None),
        ),
        out_specs=(
            P(("nodes", "feat"), None),
            P("nodes", "feat"),
            P("feat", None),
            P("feat", None),
            P("feat", None),
            P("feat", None),
        ),
        check_vma=False,
    )
```

```python
import functools
import math

import jax
import jax.numpy as jnp
from jax import lax
from jax.experimental import pallas as pl
from jax.experimental.pallas import tpu as pltpu
from jax.sharding import PartitionSpec as P

OFFSETS = (1, -1, 2, -2)
MESH = pl.DeviceIdType.MESH
F32, BF16 = jnp.float32, jnp.bfloat16
NN = (((1,), (0,)), ((), ()))
NT = (((1,), (1,)), ((), ()))


def mm(lhs, rhs, dims=NN):
    return lax.dot_general(lhs, rhs, dims, preferred_element_type=F32)


def slope_of(values, gate):
    return gate * (1.0 + values * (1.0 - gate))


def kernel(
    sizes,
    scale,
    ids_in,
    counts_in,
    lists_in,
    x_in,
    adj_in,
    w1s_in,
    w1n_in,
    w2s_in,
    w2n_in,
    up_in,
    act_out,
    fg_out,
    g1s_out,
    g1n_out,
    g2s_out,
    g2n_out,
    act_o,
    fg_o,
    g1s_o,
    g1n_o,
    g2s_o,
    g2n_o,
    ids,
    counts,
    lists,
    x_ref,
    adj,
    w1s,
    w1n,
    w2s,
    w2n,
    up,
    w1i,
    w1t,
    w2t,
    up_t,
    rdeg,
    x_own,
    x_halo_out,
    src1,
    agg1_col,
    r1,
    slope1,
    slope1_col,
    slope_halo_out,
    slope_halo_in,
    r1_halo_out,
    r1_halo_in,
    row2,
    h_own,
    h_halo_out,
    src2,
    agg2_col,
    d2,
    self2,
    u2_row,
    u2_col,
    to_halo,
    to_own,
    part,
    back2_out,
    back2_in,
    sp2_col,
    sp2_row,
    u1_row,
    u1_col,
    back1_out,
    back1_in,
    g2_out,
    g2_in,
    g2y_out,
    g2y_in,
    g2z_out,
    g2z_in,
    g2w_out,
    g2w_in,
    g2_all,
    g1y_out,
    g1y_in,
    g1z_out,
    g1z_in,
    g1_own,
    g1_all,
    feat_send,
    feat_recv,
    halo_send,
    halo_recv,
    y_send,
    y_recv,
    z_send,
    z_recv,
    cross_send,
    cross_recv,
    load_sems,
    store_sems,
):
    nodes, ny, nz, nf, nb, ns = sizes
    p = lax.axis_index("nodes")
    f = lax.axis_index("feat")
    y, z = p // nz, p % nz
    cols1, cols2 = x_own.shape[1], h_own.shape[1]
    hid = d2.shape[0]
    halo_blocks = x_halo_out.shape[1]
    total = nb + len(OFFSETS) * halo_blocks

    def feat_peer(k):
        return (p, (f + k) % nf)

    def node_peer(offset):
        return ((p + nodes + offset) % nodes, f)

    def y_peer(k):
        return (((y + k) % ny) * nz + z, f)

    def z_peer(k):
        return (y * nz + (z + k) % nz, f)

    near = 4

    def near_peer(k):
        return (y * nz + z // near * near + (z % near + k) % near, f)

    def stride_peer(k):
        return (y * nz + (z + near * k) % nz, f)

    def far_first(size):
        return sorted(range(1, size), key=lambda k: -min(k, size - k))

    loads = [
        pltpu.make_async_copy(src, dst, load_sems.at[i])
        for i, (src, dst) in enumerate(
            (
                (x_in, x_ref),
                (lists_in, lists),
                (ids_in, ids),
                (counts_in, counts),
                (adj_in, adj),
                (w1s_in, w1s),
                (w1n_in, w1n),
                (w2s_in, w2s),
                (w2n_in, w2n),
                (up_in, up),
            )
        )
    ]
    for load in loads:
        load.start()
    stores = [
        pltpu.make_async_copy(src, dst, store_sems.at[i])
        for i, (src, dst) in enumerate(
            (
                (act_o, act_out),
                (fg_o, fg_out),
                (g1s_o, g1s_out),
                (g1n_o, g1n_out),
                (g2s_o, g2s_out),
                (g2n_o, g2n_out),
            )
        )
    ]

    barrier = pltpu.get_barrier_semaphore()
    peers = (
        [node_peer(o) for o in OFFSETS]
        + [feat_peer(k) for k in range(1, nf)]
        + [y_peer(k) for k in range(1, ny)]
        + [z_peer(k) for k in range(1, nz)]
    )
    for peer in peers:
        pl.semaphore_signal(barrier, inc=1, device_id=peer, device_id_type=MESH)
    for s in range(nf):

        @pl.when(jnp.logical_or(f != y, f != s))
        def _():
            pl.semaphore_signal(barrier, inc=1, device_id=(f * nz + z, s), device_id_type=MESH)

    arrivals = len(peers) + ny - jnp.where(f == y, 1, 0)

    sent = []

    def drain():
        while sent:
            sent.pop(0).wait_send()

    def start(src, dst, ssem, rsem, peer):
        copy = pltpu.make_async_remote_copy(
            src_ref=src, dst_ref=dst, send_sem=ssem, recv_sem=rsem, device_id=peer, device_id_type=MESH
        )
        copy.start()
        sent.append(copy)
        return copy

    def feat_hop(hop, src_of, dst):
        copies = []
        for k in far_first(nf):
            g = (f + k) % nf
            copies.append(
                start(src_of(g), dst, feat_send.at[hop, k - 1], feat_recv.at[hop, k - 1], feat_peer(k))
            )
        return copies

    def halo_hop(hop, src, dst_of, sign):
        return [
            start(src.at[i], dst_of(i), halo_send.at[hop, i], halo_recv.at[hop, i], node_peer(sign * o))
            for i, o in sorted(enumerate(OFFSETS), key=lambda pair: -abs(pair[1]))
        ]

    def line_hop(hop, size, src_of, dst, sems, peer_of, me):
        return [
            start(src_of((me + k) % size), dst, sems[0].at[hop, k - 1], sems[1].at[hop, k - 1], peer_of(k))
            for k in far_first(size)
        ]

    def landed(copies):
        for copy in reversed(copies):
            copy.wait_recv()

    loads[0].wait()
    loads[1].wait()
    sent_ids = [[lists[0, h, i] for h in range(halo_blocks)] for i in range(len(OFFSETS))]
    for b in range(nb):
        x_own[b] = x_ref[:, 128 * b : 128 * (b + 1)]
    for i in range(len(OFFSETS)):
        for h in range(halo_blocks):
            x_halo_out[i, h] = x_own[sent_ids[i][h]]

    pl.semaphore_wait(barrier, arrivals)

    halo1 = halo_hop(0, x_halo_out, lambda i: src1.at[pl.ds(nb + halo_blocks * i, halo_blocks)], 1)
    x_all = feat_hop(0, lambda g: x_own, r1.at[:, f, 0])

    src1[pl.ds(0, nb)] = x_own[...]
    src1[total] = jnp.zeros((cols1, 128), BF16)
    src2[total] = jnp.zeros((cols2, 128), BF16)
    r1[:, f, 0] = x_own[...]
    for load in loads[2:5]:
        load.wait()
    targets = [
        [jnp.where(j < counts[b], ids[j, b], total) for j in range(ns)] for b in range(nb)
    ]
    for b in range(nb):
        ones = jnp.concatenate(
            [
                jnp.full((16, 128), jnp.where(targets[b][j] < total, 1.0, 0.0), F32)
                for j in range(ns)
            ],
            1,
        ).astype(BF16)
        deg = sum(mm(ones[:, 128 * j : 128 * (j + 1)], adj[b, j], NT) for j in range(ns))
        rdeg[b] = 1.0 / deg[0:8]
    for load in loads[5:]:
        load.wait()
    for g in range(nf):
        w1i[g, 0:cols1] = w1s[cols1 * g : cols1 * (g + 1)]
        w1i[g, cols1:] = w1n[cols1 * g : cols1 * (g + 1)]
    w1t[...] = w1i[...].reshape(2 * nf * cols1, hid).T.reshape(w1t.shape)

    def aggregate(src, out):
        for b in range(nb):
            total_b = sum(mm(src[targets[b][j]], adj[b, j], NT) for j in range(ns))
            out[b] = (total_b * rdeg[b][0:1]).astype(BF16)

    def dense(out, first, low, high):
        def body(b, carry):
            rows = pl.ds(pl.multiple_of(b * 128, 128), 128)
            for n in range(nb):
                tile = jnp.zeros((8, 16, 128), BF16)
                for j in range(ns):
                    here = jnp.logical_and(j < counts[b], ids[j, b] == first + n)
                    mask = jnp.full((16, 128), jnp.where(here, 1.0, 0.0), F32).astype(BF16)
                    tile = tile + adj[b, j].reshape(8, 16, 128) * mask[None]
                out[rows, 128 * n : 128 * (n + 1)] = tile.reshape(128, 128)
            return carry

        lax.fori_loop(low, high, body, 0)

    def all_blocks(u, lo, c):
        return jnp.concatenate([u[b][lo : lo + c] for b in range(nb)], 1)

    def halo_sums(u, out, c):
        sums = mm(u, to_halo[...]).astype(BF16)
        for n in range(len(OFFSETS) * halo_blocks):
            out[n // halo_blocks, n % halo_blocks] = sums[:, 128 * n : 128 * (n + 1)]

    def with_returned(back, n, c):
        acc = part[0:c, 128 * n : 128 * (n + 1)]
        for i in range(len(OFFSETS)):
            for h in range(halo_blocks):
                here = jnp.where(sent_ids[i][h] == n, 1.0, 0.0)
                acc = acc + here * back[i, h].astype(F32)
        return acc

    landed(halo1)
    aggregate(src1, agg1_col)
    agg1_all = feat_hop(1, lambda g: agg1_col, r1.at[:, f, 1])
    r1[:, f, 1] = agg1_col[...]
    dense(to_halo, nb, 0, nb // 2)
    w2t[:, 0:hid] = w2s[...].T
    w2t[:, hid:] = w2n[...].T
    up_t[...] = up[...].T
    landed(x_all)
    landed(agg1_all)
    blocks1 = [r1[b].reshape(2 * nf * cols1, 128) for b in range(nb)]
    first_cols = mm(w1t[f], jnp.concatenate(blocks1, 1))
    gate = jax.nn.sigmoid(first_cols)
    hidden_cols = (first_cols * gate).astype(BF16)
    for b in range(nb):
        h_own[b] = hidden_cols[:, 128 * b : 128 * (b + 1)]
    for i in range(len(OFFSETS)):
        for h in range(halo_blocks):
            h_halo_out[i, h] = h_own[sent_ids[i][h]]
    halo2 = halo_hop(1, h_halo_out, lambda i: src2.at[pl.ds(nb + halo_blocks * i, halo_blocks)], 1)
    slopes = slope_of(first_cols, gate)
    for b in range(nb):
        slope1_col[b] = slopes[:, 128 * b : 128 * (b + 1)]
    for i in range(len(OFFSETS)):
        for h in range(halo_blocks):
            slope_halo_out[i, h] = slope1_col[sent_ids[i][h]].astype(BF16)
            r1_halo_out[i, h] = r1[sent_ids[i][h]]
    slope_halo = halo_hop(4, slope_halo_out, lambda i: slope_halo_in.at[i], 1)
    r1_halo = halo_hop(5, r1_halo_out, lambda i: r1_halo_in.at[i], 1)
    first_pre = mm(w1t[...].reshape(hid, 2 * nf * cols1), r1[f].reshape(2 * nf * cols1, 128))
    gate = jax.nn.sigmoid(first_pre)
    row2[0:nf] = (first_pre * gate).astype(BF16).reshape(nf, cols2, 128)
    slope1[...] = slope_of(first_pre, gate)
    dense(to_halo, nb, nb // 2, nb)

    src2[pl.ds(0, nb)] = h_own[...]
    landed(halo2)
    aggregate(src2, agg2_col)
    agg2_rows = feat_hop(2, lambda g: agg2_col.at[g], row2.at[nf + f])
    row2[nf + f] = agg2_col[f]
    dense(to_own, 0, 0, nb // 2)
    landed(agg2_rows)
    rows2 = row2[...].reshape(2 * hid, 128)
    second_pre = mm(w2t[...], rows2)
    gate = jax.nn.sigmoid(second_pre)
    delta_two = (up_t[...].astype(F32) * slope_of(second_pre, gate)).astype(BF16)
    d2[...] = delta_two
    own_rdeg = rdeg[f][0:1]
    u2_row[:, 0:cols2] = (mm(w2n[...], delta_two) * own_rdeg).astype(BF16).reshape(nf, cols2, 128)
    self_two = mm(w2s[...], delta_two).astype(BF16)
    self2[...] = self_two
    u2_row[:, cols2:] = self_two.reshape(nf, cols2, 128)
    u2_cols = feat_hop(3, lambda g: u2_row.at[g], u2_col.at[f])
    u2_col[f] = u2_row[f]

    grad2 = mm(rows2, delta_two, NT).astype(BF16)
    g2_out[:, 0:cols2] = grad2[0:hid].reshape(nf, cols2, hid)
    g2_out[:, cols2:] = grad2[hid:].reshape(nf, cols2, hid)
    g2_feat = feat_hop(4, lambda g: g2_out.at[g], g2_in.at[f])
    g2_in[f] = g2_out[f]
    act_o[...] = (second_pre * gate).T.astype(BF16)
    stores[0].start()
    dense(to_own, 0, nb // 2, nb)

    landed(u2_cols)
    u2_all = all_blocks(u2_col, 0, cols2)
    halo_sums(u2_all, back2_out, cols2)
    back2 = halo_hop(2, back2_out, lambda i: back2_in.at[i], -1)
    part[...] = mm(u2_all, to_own[...])

    landed(slope_halo)
    landed(r1_halo)
    deltas, rows = [], []
    for n in range(nb):
        hidden_grad = u2_col[n][cols2:].astype(F32) + part[:, 128 * n : 128 * (n + 1)]
        deltas.append((hidden_grad * slope1_col[n]).astype(BF16))
        rows.append(r1[n].reshape(2 * nf * cols1, 128))
    for i in range(len(OFFSETS)):
        for h in range(halo_blocks):
            returned = back2_out[i, h].astype(F32) * slope_halo_in[i, h].astype(F32)
            deltas.append(returned.astype(BF16))
            rows.append(r1_halo_in[i, h].reshape(2 * nf * cols1, 128))
    copies = 128 // cols2
    grad1 = mm(
        jnp.concatenate(rows, 1), jnp.concatenate([jnp.concatenate(deltas, 1)] * copies, 0), NT
    )
    group = lax.broadcasted_iota(jnp.int32, (8, 128), 1) // cols2
    for g in range(nf):
        packed = jnp.zeros((8, 128), F32)
        for q in range(copies):
            row = 2 * cols1 * g + 8 * q
            packed = jnp.where(group == q, grad1[row : row + 8], packed)
        g1y_out[g] = packed
    y_sems, z_sems = (y_send, y_recv), (z_send, z_recv)
    g1_y = line_hop(1, ny, lambda g: g1y_out.at[g], g1y_in.at[y], y_sems, y_peer, y)
    g1y_in[y] = g1y_out[y]

    landed(g2_feat)
    g2_sum = g2_in[0].astype(F32)
    for k in range(1, nf):
        g2_sum = g2_sum + g2_in[k].astype(F32)
    for g in range(ny):
        for a in range(hid // 128):
            chunk = g2_sum[8 * g : 8 * (g + 1), 128 * a : 128 * (a + 1)]
            g2y_out[g, 8 * a : 8 * (a + 1)] = chunk.astype(BF16)
    g2_y = line_hop(0, ny, lambda g: g2y_out.at[g], g2y_in.at[y], y_sems, y_peer, y)
    g2y_in[y] = g2y_out[y]

    landed(back2)
    for n in range(nb):
        sp2_col[n] = with_returned(back2_in, n, cols2).astype(BF16)
    sp2_rows = feat_hop(5, lambda g: sp2_col.at[g], sp2_row.at[f])
    sp2_row[f] = sp2_col[f]

    landed(g1_y)
    g1z_out[...] = jnp.sum(g1y_in[...], 0)
    g1_z = line_hop(1, nz, lambda g: g1z_out, g1z_in.at[z], z_sems, z_peer, z)
    g1z_in[z] = g1z_out[...]

    landed(g2_y)
    g2z_out[...] = jnp.sum(g2y_in[...].astype(F32), 0).astype(BF16)
    g2_z = line_hop(0, near, lambda g: g2z_out, g2z_in.at[z % near], z_sems, near_peer, z % near)
    g2z_in[z % near] = g2z_out[...]

    landed(sp2_rows)
    hidden_grad = (
        self2[...].astype(F32) + sp2_row[...].reshape(hid, 128).astype(F32)
    ).astype(BF16)
    delta_one = (hidden_grad.astype(F32) * slope1[...]).astype(BF16)
    back = mm(w1i[...].reshape(2 * nf * cols1, hid), delta_one).reshape(nf, 2 * cols1, 128)
    u1_row[:, 0:cols1] = back[:, 0:cols1].astype(BF16)
    u1_row[:, cols1:] = (back[:, cols1:] * own_rdeg).astype(BF16)
    u1_cols = feat_hop(6, lambda g: u1_row.at[g], u1_col.at[f])
    u1_col[f] = u1_row[f]

    landed(g2_z)
    g2w_out[...] = jnp.sum(g2z_in[...].astype(F32), 0).astype(BF16)
    g2_w = line_hop(
        2, nz // near, lambda g: g2w_out, g2w_in.at[z // near], z_sems, stride_peer, z // near
    )
    g2w_in[z // near] = g2w_out[...]
    drain()
    landed(u1_cols)
    u1_all = all_blocks(u1_col, cols1, cols1)
    halo_sums(u1_all, back1_out, cols1)
    back1 = halo_hop(3, back1_out, lambda i: back1_in.at[i], -1)
    part[0:cols1] = mm(u1_all, to_own[...])

    landed(g1_z)
    g1_own[...] = jnp.sum(g1z_in[...], 0) * scale
    cross = [
        pltpu.make_async_remote_copy(
            src_ref=g1_own,
            dst_ref=g1_all.at[f],
            send_sem=cross_send.at[k],
            recv_sem=cross_recv.at[f],
            device_id=(((y + k) % ny) * nz + z, y),
            device_id_type=MESH,
        )
        for k in range(ny)
    ]
    for k in far_first(ny):
        cross[k].start()

    @pl.when(f != y)
    def _():
        cross[0].start()

    @pl.when(f == y)
    def _():
        g1_all[f] = g1_own[...]

    landed(g2_w)
    g2_all[y] = (jnp.sum(g2w_in[...].astype(F32), 0) * scale).astype(BF16)
    g2_back = line_hop(2, ny, lambda g: g2_all.at[y], g2_all.at[y], y_sems, y_peer, y)

    landed(back1)
    for n in range(nb):
        fg_o[:, 128 * n : 128 * (n + 1)] = (
            u1_col[n][0:cols1].astype(F32) + with_returned(back1_in, n, cols1)
        ).astype(BF16)
    stores[1].start()

    landed(g2_back)
    for g in range(ny):
        out = g2s_o if 8 * g < cols2 else g2n_o
        row = 8 * g % cols2
        chunk = g2_all[g].astype(F32)
        for a in range(hid // 128):
            out[row : row + 8, 128 * a : 128 * (a + 1)] = chunk[8 * a : 8 * (a + 1)]
    stores[4].start()
    stores[5].start()

    drain()
    for s in range(nf):

        @pl.when(jnp.logical_or(f != y, f != s))
        def _():
            pltpu.make_async_remote_copy(
                src_ref=g1_own,
                dst_ref=g1_all.at[s],
                send_sem=cross_send.at[0],
                recv_sem=cross_recv.at[s],
                device_id=(f * nz + z, s),
                device_id_type=MESH,
            ).wait_recv()

    for q in range(copies):
        out = g1s_o if 8 * q < cols1 else g1n_o
        row = 8 * q % cols1
        for a in range(hid // 128):
            wide = jnp.zeros((8, 128), F32)
            for t in range(copies):
                tile = g1_all[a * copies + t]
                shift = (t - q) * cols2 % 128
                wide = jnp.where(group == t, pltpu.roll(tile, shift, 1) if shift else tile, wide)
            out[row : row + 8, 128 * a : 128 * (a + 1)] = wide
    stores[2].start()
    stores[3].start()

    for k in range(1, ny):
        cross[k].wait_send()

    @pl.when(f != y)
    def _():
        cross[0].wait_send()

    for copy in stores:
        copy.wait()


def store(count, *refs):
    ins, outs, held = refs[:count], refs[count : 2 * count], refs[2 * count : 3 * count]
    sems = refs[-1]
    fetch = [pltpu.make_async_copy(ins[i], held[i], sems.at[0, i]) for i in range(count)]
    write = [pltpu.make_async_copy(held[i], outs[i], sems.at[1, i]) for i in range(count)]
    for copy in fetch:
        copy.start()
    for first, second in zip(fetch, write):
        first.wait()
        second.start()
    for copy in write:
        copy.wait()


def on_device(
    features,
    adjacency,
    source_ids,
    counts,
    send_lists,
    first_self,
    first_neighbour,
    second_self,
    second_neighbour,
    upstream,
):
    nodes, nf = lax.axis_size("nodes"), lax.axis_size("feat")
    ny = 8
    nz = nodes // ny
    nb, ns, bs = adjacency.shape[0], adjacency.shape[1], adjacency.shape[2]
    hs = send_lists.shape[2]
    total = nb + len(OFFSETS) * hs
    c1 = features.shape[1]
    hid = upstream.shape[1]
    c2 = hid // nf
    noff = len(OFFSETS)
    scale = 1.0 / math.sqrt(nb * bs * nodes)
    hbm = pl.BlockSpec(memory_space=pltpu.HBM)
    scratch = [
        ((bs, hid), BF16),
        ((c1, nb * bs), BF16),
        ((c1, hid), F32),
        ((c1, hid), F32),
        ((c2, hid), F32),
        ((c2, hid), F32),
        ((c1, nb * bs), BF16),
        (adjacency.shape, BF16),
        (first_self.shape, BF16),
        (first_neighbour.shape, BF16),
        (second_self.shape, BF16),
        (second_neighbour.shape, BF16),
        (upstream.shape, BF16),
        ((nf, 2 * c1, hid), BF16),
        ((nf, c2, 2 * nf * c1), BF16),
        ((hid, 2 * hid), BF16),
        ((hid, bs), BF16),
        ((nb, 8, bs), F32),
        ((nb, c1, bs), BF16),
        ((noff, hs, c1, bs), BF16),
        ((total + 1, c1, bs), BF16),
        ((nb, c1, bs), BF16),
        ((nb, nf, 2, c1, bs), BF16),
        ((hid, bs), F32),
        ((nb, c2, bs), F32),
        ((noff, hs, c2, bs), BF16),
        ((noff, hs, c2, bs), BF16),
        ((noff, hs, nf, 2, c1, bs), BF16),
        ((noff, hs, nf, 2, c1, bs), BF16),
        ((2 * nf, c2, bs), BF16),
        ((nb, c2, bs), BF16),
        ((noff, hs, c2, bs), BF16),
        ((total + 1, c2, bs), BF16),
        ((nb, c2, bs), BF16),
        ((hid, bs), BF16),
        ((hid, bs), BF16),
        ((nf, 2 * c2, bs), BF16),
        ((nb, 2 * c2, bs), BF16),
        ((nb * bs, noff * hs * bs), BF16),
        ((nb * bs, nb * bs), BF16),
        ((c2, nb * bs), F32),
        ((noff, hs, c2, bs), BF16),
        ((noff, hs, c2, bs), BF16),
        ((nb, c2, bs), BF16),
        ((nf, c2, bs), BF16),
        ((nf, 2 * c1, bs), BF16),
        ((nb, 2 * c1, bs), BF16),
        ((noff, hs, c1, bs), BF16),
        ((noff, hs, c1, bs), BF16),
        ((nf, 2 * c2, hid), BF16),
        ((nf, 2 * c2, hid), BF16),
        ((ny, 16, 128), BF16),
        ((ny, 16, 128), BF16),
        ((16, 128), BF16),
        ((4, 16, 128), BF16),
        ((16, 128), BF16),
        ((nz // 4, 16, 128), BF16),
        ((ny, 16, 128), BF16),
        ((ny, 8, 128), F32),
        ((ny, 8, 128), F32),
        ((8, 128), F32),
        ((nz, 8, 128), F32),
        ((8, 128), F32),
        ((nf, 8, 128), F32),
    ]
    dma = pltpu.SemaphoreType.DMA
    outs = pl.pallas_call(
        functools.partial(kernel, (nodes, ny, nz, nf, nb, ns), scale),
        out_shape=(
            jax.ShapeDtypeStruct((bs, hid), BF16),
            jax.ShapeDtypeStruct((c1, nb * bs), BF16),
            jax.ShapeDtypeStruct((c1, hid), F32),
            jax.ShapeDtypeStruct((c1, hid), F32),
            jax.ShapeDtypeStruct((c2, hid), F32),
            jax.ShapeDtypeStruct((c2, hid), F32),
        ),
        in_specs=[hbm] * 10,
        out_specs=(hbm,) * 6,
        scratch_shapes=[pltpu.VMEM(shape, kind) for shape, kind in scratch[:6]]
        + [
            pltpu.SMEM((ns, nb), jnp.int32),
            pltpu.SMEM((nb,), jnp.int32),
            pltpu.SMEM((1, hs, noff), jnp.int32),
        ]
        + [pltpu.VMEM(shape, kind) for shape, kind in scratch[6:]]
        + [
            dma((7, nf - 1)),
            dma((7, nf - 1)),
            dma((6, noff)),
            dma((6, noff)),
            dma((3, ny - 1)),
            dma((3, ny - 1)),
            dma((3, nz - 1)),
            dma((3, nz - 1)),
            dma((ny,)),
            dma((nf,)),
            dma((10,)),
            dma((6,)),
        ],
        compiler_params=pltpu.CompilerParams(
            collective_id=0, has_side_effects=True, vmem_limit_bytes=60 * 1024 * 1024
        ),
    )(
        source_ids.T,
        counts,
        send_lists.transpose(0, 2, 1),
        features.T,
        adjacency,
        first_self,
        first_neighbour,
        second_self,
        second_neighbour,
        upstream,
    )
    outs = pl.pallas_call(
        functools.partial(store, len(outs)),
        out_shape=tuple(jax.ShapeDtypeStruct(o.shape, o.dtype) for o in outs),
        in_specs=[hbm] * len(outs),
        out_specs=(hbm,) * len(outs),
        scratch_shapes=[pltpu.VMEM(o.shape, o.dtype) for o in outs] + [dma((2, len(outs)))],
        compiler_params=pltpu.CompilerParams(vmem_limit_bytes=60 * 1024 * 1024),
    )(*outs)
    return (outs[0], outs[1].T) + tuple(outs[2:])


def solution(mesh):
    return jax.shard_map(
        on_device,
        mesh=mesh,
        in_specs=(
            P("nodes", "feat"),
            P("nodes", None, None, None),
            P("nodes", None),
            P("nodes"),
            P("nodes", None, None),
            P(),
            P(),
            P(),
            P(),
            P(("nodes", "feat"), None),
        ),
        out_specs=(
            P(("nodes", "feat"), None),
            P("nodes", "feat"),
            P("feat", None),
            P("feat", None),
            P("feat", None),
            P("feat", None),
        ),
        check_vma=False,
    )
```

```python
import functools
import math

import jax
import jax.numpy as jnp
from jax import lax
from jax.experimental import pallas as pl
from jax.experimental.pallas import tpu as pltpu
from jax.sharding import PartitionSpec as P

OFFSETS = (1, -1, 2, -2)
MESH = pl.DeviceIdType.MESH
F32, BF16 = jnp.float32, jnp.bfloat16
NN = (((1,), (0,)), ((), ()))
NT = (((1,), (1,)), ((), ()))


def mm(lhs, rhs, dims=NN):
    return lax.dot_general(lhs, rhs, dims, preferred_element_type=F32)


def slope_of(values, gate):
    return gate * (1.0 + values * (1.0 - gate))


def kernel(
    sizes,
    scale,
    ids_in,
    counts_in,
    lists_in,
    x_in,
    adj_in,
    w1s_in,
    w1n_in,
    w2s_in,
    w2n_in,
    up_in,
    act_out,
    fg_out,
    g1s_out,
    g1n_out,
    g2s_out,
    g2n_out,
    act_o,
    fg_o,
    g1s_o,
    g1n_o,
    g2s_o,
    g2n_o,
    ids,
    counts,
    lists,
    x_ref,
    adj,
    w1s,
    w1n,
    w2s,
    w2n,
    up,
    w1i,
    w1t,
    w2t,
    up_t,
    rdeg,
    x_own,
    x_halo_out,
    src1,
    agg1_col,
    r1,
    slope1,
    slope1_col,
    slope_halo_out,
    slope_halo_in,
    r1_halo_out,
    r1_halo_in,
    row2,
    h_own,
    h_halo_out,
    src2,
    agg2_col,
    d2,
    self2,
    u2_row,
    u2_col,
    to_halo,
    to_own,
    part,
    back2_out,
    back2_in,
    sp2_col,
    sp2_row,
    u1_row,
    u1_col,
    back1_out,
    back1_in,
    g2_out,
    g2_in,
    g2y_out,
    g2y_in,
    g2z_out,
    g2z_in,
    g2_all,
    g1y_out,
    g1y_in,
    g1z_out,
    g1z_in,
    g1_own,
    g1_all,
    feat_send,
    feat_recv,
    halo_send,
    halo_recv,
    y_send,
    y_recv,
    z_send,
    z_recv,
    cross_send,
    cross_recv,
    load_sems,
    store_sems,
):
    nodes, ny, nz, nf, nb, ns = sizes
    p = lax.axis_index("nodes")
    f = lax.axis_index("feat")
    y, z = p // nz, p % nz
    cols1, cols2 = x_own.shape[1], h_own.shape[1]
    hid = d2.shape[0]
    halo_blocks = x_halo_out.shape[1]
    total = nb + len(OFFSETS) * halo_blocks

    def feat_peer(k):
        return (p, (f + k) % nf)

    def node_peer(offset):
        return ((p + nodes + offset) % nodes, f)

    def y_peer(k):
        return (((y + k) % ny) * nz + z, f)

    def z_peer(k):
        return (y * nz + (z + k) % nz, f)

    def far_first(size):
        return sorted(range(1, size), key=lambda k: -min(k, size - k))

    loads = [
        pltpu.make_async_copy(src, dst, load_sems.at[i])
        for i, (src, dst) in enumerate(
            (
                (x_in, x_ref),
                (lists_in, lists),
                (ids_in, ids),
                (counts_in, counts),
                (adj_in, adj),
                (w1s_in, w1s),
                (w1n_in, w1n),
                (w2s_in, w2s),
                (w2n_in, w2n),
                (up_in, up),
            )
        )
    ]
    for load in loads[:2]:
        load.start()
    stores = [
        pltpu.make_async_copy(src, dst, store_sems.at[i])
        for i, (src, dst) in enumerate(
            (
                (act_o, act_out),
                (fg_o, fg_out),
                (g1s_o, g1s_out),
                (g1n_o, g1n_out),
                (g2s_o, g2s_out),
                (g2n_o, g2n_out),
            )
        )
    ]

    barrier = pltpu.get_barrier_semaphore()
    peers = (
        [node_peer(o) for o in OFFSETS]
        + [feat_peer(k) for k in range(1, nf)]
        + [y_peer(k) for k in range(1, ny)]
        + [z_peer(k) for k in range(1, nz)]
    )
    for peer in peers:
        pl.semaphore_signal(barrier, inc=1, device_id=peer, device_id_type=MESH)
    for s in range(nf):

        @pl.when(jnp.logical_or(f != y, f != s))
        def _():
            pl.semaphore_signal(barrier, inc=1, device_id=(f * nz + z, s), device_id_type=MESH)

    arrivals = len(peers) + ny - jnp.where(f == y, 1, 0)

    sent = []

    def drain():
        while sent:
            sent.pop(0).wait_send()

    def start(src, dst, ssem, rsem, peer):
        copy = pltpu.make_async_remote_copy(
            src_ref=src, dst_ref=dst, send_sem=ssem, recv_sem=rsem, device_id=peer, device_id_type=MESH
        )
        copy.start()
        sent.append(copy)
        return copy

    def feat_hop(hop, src_of, dst):
        copies = []
        for k in far_first(nf):
            g = (f + k) % nf
            copies.append(
                start(src_of(g), dst, feat_send.at[hop, k - 1], feat_recv.at[hop, k - 1], feat_peer(k))
            )
        return copies

    def halo_hop(hop, src, dst_of, sign):
        return [
            start(src.at[i], dst_of(i), halo_send.at[hop, i], halo_recv.at[hop, i], node_peer(sign * o))
            for i, o in sorted(enumerate(OFFSETS), key=lambda pair: -abs(pair[1]))
        ]

    def line_hop(hop, size, src_of, dst, sems, peer_of, me):
        return [
            start(src_of((me + k) % size), dst, sems[0].at[hop, k - 1], sems[1].at[hop, k - 1], peer_of(k))
            for k in far_first(size)
        ]

    def landed(copies):
        for copy in reversed(copies):
            copy.wait_recv()

    loads[0].wait()
    loads[1].wait()
    sent_ids = [[lists[0, h, i] for h in range(halo_blocks)] for i in range(len(OFFSETS))]
    for b in range(nb):
        x_own[b] = x_ref[:, 128 * b : 128 * (b + 1)]
    for i in range(len(OFFSETS)):
        for h in range(halo_blocks):
            x_halo_out[i, h] = x_own[sent_ids[i][h]]

    pl.semaphore_wait(barrier, arrivals)

    halo1 = halo_hop(0, x_halo_out, lambda i: src1.at[pl.ds(nb + halo_blocks * i, halo_blocks)], 1)
    x_all = feat_hop(0, lambda g: x_own, r1.at[:, f, 0])
    for load in loads[2:]:
        load.start()

    src1[pl.ds(0, nb)] = x_own[...]
    src1[total] = jnp.zeros((cols1, 128), BF16)
    src2[total] = jnp.zeros((cols2, 128), BF16)
    r1[:, f, 0] = x_own[...]
    for load in loads[2:5]:
        load.wait()
    targets = [
        [jnp.where(j < counts[b], ids[j, b], total) for j in range(ns)] for b in range(nb)
    ]
    for b in range(nb):
        ones = jnp.concatenate(
            [
                jnp.full((16, 128), jnp.where(targets[b][j] < total, 1.0, 0.0), F32)
                for j in range(ns)
            ],
            1,
        ).astype(BF16)
        deg = sum(mm(ones[:, 128 * j : 128 * (j + 1)], adj[b, j], NT) for j in range(ns))
        rdeg[b] = 1.0 / deg[0:8]
    for load in loads[5:]:
        load.wait()
    for g in range(nf):
        w1i[g, 0:cols1] = w1s[cols1 * g : cols1 * (g + 1)]
        w1i[g, cols1:] = w1n[cols1 * g : cols1 * (g + 1)]
    w1t[...] = w1i[...].reshape(2 * nf * cols1, hid).T.reshape(w1t.shape)

    def aggregate(src, out):
        for b in range(nb):
            total_b = sum(mm(src[targets[b][j]], adj[b, j], NT) for j in range(ns))
            out[b] = (total_b * rdeg[b][0:1]).astype(BF16)

    def dense(out, first, low, high):
        def body(b, carry):
            rows = pl.ds(pl.multiple_of(b * 128, 128), 128)
            for n in range(nb):
                tile = jnp.zeros((8, 16, 128), BF16)
                for j in range(ns):
                    here = jnp.logical_and(j < counts[b], ids[j, b] == first + n)
                    mask = jnp.full((16, 128), jnp.where(here, 1.0, 0.0), F32).astype(BF16)
                    tile = tile + adj[b, j].reshape(8, 16, 128) * mask[None]
                out[rows, 128 * n : 128 * (n + 1)] = tile.reshape(128, 128)
            return carry

        lax.fori_loop(low, high, body, 0)

    def all_blocks(u, lo, c):
        return jnp.concatenate([u[b][lo : lo + c] for b in range(nb)], 1)

    def halo_sums(u, out, c):
        sums = mm(u, to_halo[...]).astype(BF16)
        for n in range(len(OFFSETS) * halo_blocks):
            out[n // halo_blocks, n % halo_blocks] = sums[:, 128 * n : 128 * (n + 1)]

    def with_returned(back, n, c):
        acc = part[0:c, 128 * n : 128 * (n + 1)]
        for i in range(len(OFFSETS)):
            for h in range(halo_blocks):
                here = jnp.where(sent_ids[i][h] == n, 1.0, 0.0)
                acc = acc + here * back[i, h].astype(F32)
        return acc

    landed(halo1)
    aggregate(src1, agg1_col)
    agg1_all = feat_hop(1, lambda g: agg1_col, r1.at[:, f, 1])
    r1[:, f, 1] = agg1_col[...]
    dense(to_halo, nb, 0, nb // 2)
    w2t[:, 0:hid] = w2s[...].T
    w2t[:, hid:] = w2n[...].T
    up_t[...] = up[...].T
    landed(x_all)
    landed(agg1_all)
    blocks1 = [r1[b].reshape(2 * nf * cols1, 128) for b in range(nb)]
    first_cols = mm(w1t[f], jnp.concatenate(blocks1, 1))
    gate = jax.nn.sigmoid(first_cols)
    hidden_cols = (first_cols * gate).astype(BF16)
    for b in range(nb):
        h_own[b] = hidden_cols[:, 128 * b : 128 * (b + 1)]
    for i in range(len(OFFSETS)):
        for h in range(halo_blocks):
            h_halo_out[i, h] = h_own[sent_ids[i][h]]
    halo2 = halo_hop(1, h_halo_out, lambda i: src2.at[pl.ds(nb + halo_blocks * i, halo_blocks)], 1)
    slopes = slope_of(first_cols, gate)
    for b in range(nb):
        slope1_col[b] = slopes[:, 128 * b : 128 * (b + 1)]
    for i in range(len(OFFSETS)):
        for h in range(halo_blocks):
            slope_halo_out[i, h] = slope1_col[sent_ids[i][h]].astype(BF16)
            r1_halo_out[i, h] = r1[sent_ids[i][h]]
    slope_halo = halo_hop(4, slope_halo_out, lambda i: slope_halo_in.at[i], 1)
    r1_halo = halo_hop(5, r1_halo_out, lambda i: r1_halo_in.at[i], 1)
    first_pre = mm(w1t[...].reshape(hid, 2 * nf * cols1), r1[f].reshape(2 * nf * cols1, 128))
    gate = jax.nn.sigmoid(first_pre)
    row2[0:nf] = (first_pre * gate).astype(BF16).reshape(nf, cols2, 128)
    slope1[...] = slope_of(first_pre, gate)
    dense(to_halo, nb, nb // 2, nb)

    src2[pl.ds(0, nb)] = h_own[...]
    landed(halo2)
    aggregate(src2, agg2_col)
    agg2_rows = feat_hop(2, lambda g: agg2_col.at[g], row2.at[nf + f])
    row2[nf + f] = agg2_col[f]
    dense(to_own, 0, 0, nb // 2)
    landed(agg2_rows)
    rows2 = row2[...].reshape(2 * hid, 128)
    second_pre = mm(w2t[...], rows2)
    gate = jax.nn.sigmoid(second_pre)
    delta_two = (up_t[...].astype(F32) * slope_of(second_pre, gate)).astype(BF16)
    d2[...] = delta_two
    own_rdeg = rdeg[f][0:1]
    u2_row[:, 0:cols2] = (mm(w2n[...], delta_two) * own_rdeg).astype(BF16).reshape(nf, cols2, 128)
    self_two = mm(w2s[...], delta_two).astype(BF16)
    self2[...] = self_two
    u2_row[:, cols2:] = self_two.reshape(nf, cols2, 128)
    u2_cols = feat_hop(3, lambda g: u2_row.at[g], u2_col.at[f])
    u2_col[f] = u2_row[f]

    grad2 = mm(rows2, delta_two, NT).astype(BF16)
    g2_out[:, 0:cols2] = grad2[0:hid].reshape(nf, cols2, hid)
    g2_out[:, cols2:] = grad2[hid:].reshape(nf, cols2, hid)
    g2_feat = feat_hop(4, lambda g: g2_out.at[g], g2_in.at[f])
    g2_in[f] = g2_out[f]
    act_o[...] = (second_pre * gate).T.astype(BF16)
    stores[0].start()
    dense(to_own, 0, nb // 2, nb)

    landed(u2_cols)
    u2_all = all_blocks(u2_col, 0, cols2)
    halo_sums(u2_all, back2_out, cols2)
    back2 = halo_hop(2, back2_out, lambda i: back2_in.at[i], -1)
    part[...] = mm(u2_all, to_own[...])

    landed(slope_halo)
    landed(r1_halo)
    deltas, rows = [], []
    for n in range(nb):
        hidden_grad = u2_col[n][cols2:].astype(F32) + part[:, 128 * n : 128 * (n + 1)]
        deltas.append((hidden_grad * slope1_col[n]).astype(BF16))
        rows.append(r1[n].reshape(2 * nf * cols1, 128))
    for i in range(len(OFFSETS)):
        for h in range(halo_blocks):
            returned = back2_out[i, h].astype(F32) * slope_halo_in[i, h].astype(F32)
            deltas.append(returned.astype(BF16))
            rows.append(r1_halo_in[i, h].reshape(2 * nf * cols1, 128))
    copies = 128 // cols2
    grad1 = mm(
        jnp.concatenate(rows, 1), jnp.concatenate([jnp.concatenate(deltas, 1)] * copies, 0), NT
    )
    group = lax.broadcasted_iota(jnp.int32, (8, 128), 1) // cols2
    for g in range(nf):
        packed = jnp.zeros((8, 128), F32)
        for q in range(copies):
            row = 2 * cols1 * g + 8 * q
            packed = jnp.where(group == q, grad1[row : row + 8], packed)
        g1y_out[g] = packed
    y_sems, z_sems = (y_send, y_recv), (z_send, z_recv)
    g1_y = line_hop(1, ny, lambda g: g1y_out.at[g], g1y_in.at[y], y_sems, y_peer, y)
    g1y_in[y] = g1y_out[y]

    landed(g2_feat)
    g2_sum = g2_in[0].astype(F32)
    for k in range(1, nf):
        g2_sum = g2_sum + g2_in[k].astype(F32)
    for g in range(ny):
        for a in range(hid // 128):
            chunk = g2_sum[8 * g : 8 * (g + 1), 128 * a : 128 * (a + 1)]
            g2y_out[g, 8 * a : 8 * (a + 1)] = chunk.astype(BF16)
    g2_y = line_hop(0, ny, lambda g: g2y_out.at[g], g2y_in.at[y], y_sems, y_peer, y)
    g2y_in[y] = g2y_out[y]

    landed(back2)
    for n in range(nb):
        sp2_col[n] = with_returned(back2_in, n, cols2).astype(BF16)
    sp2_rows = feat_hop(5, lambda g: sp2_col.at[g], sp2_row.at[f])
    sp2_row[f] = sp2_col[f]

    landed(g1_y)
    g1z_out[...] = jnp.sum(g1y_in[...], 0)
    g1_z = line_hop(1, nz, lambda g: g1z_out, g1z_in.at[z], z_sems, z_peer, z)
    g1z_in[z] = g1z_out[...]

    landed(g2_y)
    g2z_out[...] = jnp.sum(g2y_in[...].astype(F32), 0).astype(BF16)
    g2_z = line_hop(0, nz, lambda g: g2z_out, g2z_in.at[z], z_sems, z_peer, z)
    g2z_in[z] = g2z_out[...]

    landed(sp2_rows)
    hidden_grad = (
        self2[...].astype(F32) + sp2_row[...].reshape(hid, 128).astype(F32)
    ).astype(BF16)
    delta_one = (hidden_grad.astype(F32) * slope1[...]).astype(BF16)
    back = mm(w1i[...].reshape(2 * nf * cols1, hid), delta_one).reshape(nf, 2 * cols1, 128)
    u1_row[:, 0:cols1] = back[:, 0:cols1].astype(BF16)
    u1_row[:, cols1:] = (back[:, cols1:] * own_rdeg).astype(BF16)
    u1_cols = feat_hop(6, lambda g: u1_row.at[g], u1_col.at[f])
    u1_col[f] = u1_row[f]

    drain()
    landed(u1_cols)
    u1_all = all_blocks(u1_col, cols1, cols1)
    halo_sums(u1_all, back1_out, cols1)
    back1 = halo_hop(3, back1_out, lambda i: back1_in.at[i], -1)
    part[0:cols1] = mm(u1_all, to_own[...])

    landed(g1_z)
    g1_own[...] = jnp.sum(g1z_in[...], 0) * scale
    cross = [
        pltpu.make_async_remote_copy(
            src_ref=g1_own,
            dst_ref=g1_all.at[f],
            send_sem=cross_send.at[k],
            recv_sem=cross_recv.at[f],
            device_id=(((y + k) % ny) * nz + z, y),
            device_id_type=MESH,
        )
        for k in range(ny)
    ]
    for k in far_first(ny):
        cross[k].start()

    @pl.when(f != y)
    def _():
        cross[0].start()

    @pl.when(f == y)
    def _():
        g1_all[f] = g1_own[...]

    landed(g2_z)
    g2_all[y] = (jnp.sum(g2z_in[...].astype(F32), 0) * scale).astype(BF16)
    g2_back = line_hop(2, ny, lambda g: g2_all.at[y], g2_all.at[y], y_sems, y_peer, y)

    landed(back1)
    for n in range(nb):
        fg_o[:, 128 * n : 128 * (n + 1)] = (
            u1_col[n][0:cols1].astype(F32) + with_returned(back1_in, n, cols1)
        ).astype(BF16)
    stores[1].start()

    landed(g2_back)
    for g in range(ny):
        out = g2s_o if 8 * g < cols2 else g2n_o
        row = 8 * g % cols2
        chunk = g2_all[g].astype(F32)
        for a in range(hid // 128):
            out[row : row + 8, 128 * a : 128 * (a + 1)] = chunk[8 * a : 8 * (a + 1)]
    stores[4].start()
    stores[5].start()

    drain()
    for s in range(nf):

        @pl.when(jnp.logical_or(f != y, f != s))
        def _():
            pltpu.make_async_remote_copy(
                src_ref=g1_own,
                dst_ref=g1_all.at[s],
                send_sem=cross_send.at[0],
                recv_sem=cross_recv.at[s],
                device_id=(f * nz + z, s),
                device_id_type=MESH,
            ).wait_recv()

    for q in range(copies):
        out = g1s_o if 8 * q < cols1 else g1n_o
        row = 8 * q % cols1
        for a in range(hid // 128):
            wide = jnp.zeros((8, 128), F32)
            for t in range(copies):
                tile = g1_all[a * copies + t]
                shift = (t - q) * cols2 % 128
                wide = jnp.where(group == t, pltpu.roll(tile, shift, 1) if shift else tile, wide)
            out[row : row + 8, 128 * a : 128 * (a + 1)] = wide
    stores[2].start()
    stores[3].start()

    for k in range(1, ny):
        cross[k].wait_send()

    @pl.when(f != y)
    def _():
        cross[0].wait_send()

    for copy in stores:
        copy.wait()


def store(count, *refs):
    ins, outs, held = refs[:count], refs[count : 2 * count], refs[2 * count : 3 * count]
    sems = refs[-1]
    fetch = [pltpu.make_async_copy(ins[i], held[i], sems.at[0, i]) for i in range(count)]
    write = [pltpu.make_async_copy(held[i], outs[i], sems.at[1, i]) for i in range(count)]
    for copy in fetch:
        copy.start()
    for first, second in zip(fetch, write):
        first.wait()
        second.start()
    for copy in write:
        copy.wait()


def on_device(
    features,
    adjacency,
    source_ids,
    counts,
    send_lists,
    first_self,
    first_neighbour,
    second_self,
    second_neighbour,
    upstream,
):
    nodes, nf = lax.axis_size("nodes"), lax.axis_size("feat")
    ny = 8
    nz = nodes // ny
    nb, ns, bs = adjacency.shape[0], adjacency.shape[1], adjacency.shape[2]
    hs = send_lists.shape[2]
    total = nb + len(OFFSETS) * hs
    c1 = features.shape[1]
    hid = upstream.shape[1]
    c2 = hid // nf
    noff = len(OFFSETS)
    scale = 1.0 / math.sqrt(nb * bs * nodes)
    hbm = pl.BlockSpec(memory_space=pltpu.HBM)
    scratch = [
        ((bs, hid), BF16),
        ((c1, nb * bs), BF16),
        ((c1, hid), F32),
        ((c1, hid), F32),
        ((c2, hid), F32),
        ((c2, hid), F32),
        ((c1, nb * bs), BF16),
        (adjacency.shape, BF16),
        (first_self.shape, BF16),
        (first_neighbour.shape, BF16),
        (second_self.shape, BF16),
        (second_neighbour.shape, BF16),
        (upstream.shape, BF16),
        ((nf, 2 * c1, hid), BF16),
        ((nf, c2, 2 * nf * c1), BF16),
        ((hid, 2 * hid), BF16),
        ((hid, bs), BF16),
        ((nb, 8, bs), F32),
        ((nb, c1, bs), BF16),
        ((noff, hs, c1, bs), BF16),
        ((total + 1, c1, bs), BF16),
        ((nb, c1, bs), BF16),
        ((nb, nf, 2, c1, bs), BF16),
        ((hid, bs), F32),
        ((nb, c2, bs), F32),
        ((noff, hs, c2, bs), BF16),
        ((noff, hs, c2, bs), BF16),
        ((noff, hs, nf, 2, c1, bs), BF16),
        ((noff, hs, nf, 2, c1, bs), BF16),
        ((2 * nf, c2, bs), BF16),
        ((nb, c2, bs), BF16),
        ((noff, hs, c2, bs), BF16),
        ((total + 1, c2, bs), BF16),
        ((nb, c2, bs), BF16),
        ((hid, bs), BF16),
        ((hid, bs), BF16),
        ((nf, 2 * c2, bs), BF16),
        ((nb, 2 * c2, bs), BF16),
        ((nb * bs, noff * hs * bs), BF16),
        ((nb * bs, nb * bs), BF16),
        ((c2, nb * bs), F32),
        ((noff, hs, c2, bs), BF16),
        ((noff, hs, c2, bs), BF16),
        ((nb, c2, bs), BF16),
        ((nf, c2, bs), BF16),
        ((nf, 2 * c1, bs), BF16),
        ((nb, 2 * c1, bs), BF16),
        ((noff, hs, c1, bs), BF16),
        ((noff, hs, c1, bs), BF16),
        ((nf, 2 * c2, hid), BF16),
        ((nf, 2 * c2, hid), BF16),
        ((ny, 16, 128), BF16),
        ((ny, 16, 128), BF16),
        ((16, 128), BF16),
        ((nz, 16, 128), BF16),
        ((ny, 16, 128), BF16),
        ((ny, 8, 128), F32),
        ((ny, 8, 128), F32),
        ((8, 128), F32),
        ((nz, 8, 128), F32),
        ((8, 128), F32),
        ((nf, 8, 128), F32),
    ]
    dma = pltpu.SemaphoreType.DMA
    outs = pl.pallas_call(
        functools.partial(kernel, (nodes, ny, nz, nf, nb, ns), scale),
        out_shape=(
            jax.ShapeDtypeStruct((bs, hid), BF16),
            jax.ShapeDtypeStruct((c1, nb * bs), BF16),
            jax.ShapeDtypeStruct((c1, hid), F32),
            jax.ShapeDtypeStruct((c1, hid), F32),
            jax.ShapeDtypeStruct((c2, hid), F32),
            jax.ShapeDtypeStruct((c2, hid), F32),
        ),
        in_specs=[hbm] * 10,
        out_specs=(hbm,) * 6,
        scratch_shapes=[pltpu.VMEM(shape, kind) for shape, kind in scratch[:6]]
        + [
            pltpu.SMEM((ns, nb), jnp.int32),
            pltpu.SMEM((nb,), jnp.int32),
            pltpu.SMEM((1, hs, noff), jnp.int32),
        ]
        + [pltpu.VMEM(shape, kind) for shape, kind in scratch[6:]]
        + [
            dma((7, nf - 1)),
            dma((7, nf - 1)),
            dma((6, noff)),
            dma((6, noff)),
            dma((3, ny - 1)),
            dma((3, ny - 1)),
            dma((2, nz - 1)),
            dma((2, nz - 1)),
            dma((ny,)),
            dma((nf,)),
            dma((10,)),
            dma((6,)),
        ],
        compiler_params=pltpu.CompilerParams(
            collective_id=0, has_side_effects=True, vmem_limit_bytes=60 * 1024 * 1024
        ),
    )(
        source_ids.T,
        counts,
        send_lists.transpose(0, 2, 1),
        features.T,
        adjacency,
        first_self,
        first_neighbour,
        second_self,
        second_neighbour,
        upstream,
    )
    outs = pl.pallas_call(
        functools.partial(store, len(outs)),
        out_shape=tuple(jax.ShapeDtypeStruct(o.shape, o.dtype) for o in outs),
        in_specs=[hbm] * len(outs),
        out_specs=(hbm,) * len(outs),
        scratch_shapes=[pltpu.VMEM(o.shape, o.dtype) for o in outs] + [dma((2, len(outs)))],
        compiler_params=pltpu.CompilerParams(vmem_limit_bytes=60 * 1024 * 1024),
    )(*outs)
    return (outs[0], outs[1].T) + tuple(outs[2:])


def solution(mesh):
    return jax.shard_map(
        on_device,
        mesh=mesh,
        in_specs=(
            P("nodes", "feat"),
            P("nodes", None, None, None),
            P("nodes", None),
            P("nodes"),
            P("nodes", None, None),
            P(),
            P(),
            P(),
            P(),
            P(("nodes", "feat"), None),
        ),
        out_specs=(
            P(("nodes", "feat"), None),
            P("nodes", "feat"),
            P("feat", None),
            P("feat", None),
            P("feat", None),
            P("feat", None),
        ),
        check_vma=False,
    )
```

```python
import functools
import math

import jax
import jax.numpy as jnp
from jax import lax
from jax.experimental import pallas as pl
from jax.experimental.pallas import tpu as pltpu
from jax.sharding import PartitionSpec as P

OFFSETS = (1, -1, 2, -2)
MESH = pl.DeviceIdType.MESH
F32, BF16 = jnp.float32, jnp.bfloat16
NN = (((1,), (0,)), ((), ()))
NT = (((1,), (1,)), ((), ()))


def mm(lhs, rhs, dims=NN):
    return lax.dot_general(lhs, rhs, dims, preferred_element_type=F32)


def slope_of(values, gate):
    return gate * (1.0 + values * (1.0 - gate))


def kernel(
    sizes,
    scale,
    ids_in,
    counts_in,
    lists_in,
    x_in,
    adj_in,
    w1s_in,
    w1n_in,
    w2s_in,
    w2n_in,
    up_in,
    act_out,
    fg_out,
    g1s_out,
    g1n_out,
    g2s_out,
    g2n_out,
    act_o,
    fg_o,
    g1s_o,
    g1n_o,
    g2s_o,
    g2n_o,
    ids,
    counts,
    lists,
    x_ref,
    adj,
    w1s,
    w1n,
    w2s,
    w2n,
    up,
    w1i,
    w1t,
    w2t,
    up_t,
    rdeg,
    x_own,
    x_halo_out,
    src1,
    agg1_col,
    r1,
    slope1,
    slope1_col,
    slope_halo_out,
    slope_halo_in,
    r1_halo_out,
    r1_halo_in,
    row2,
    h_own,
    h_halo_out,
    src2,
    agg2_col,
    d2,
    self2,
    u2_row,
    u2_col,
    to_halo,
    to_own,
    part,
    back2_out,
    back2_in,
    sp2_col,
    sp2_row,
    u1_row,
    u1_col,
    back1_out,
    back1_in,
    g2_out,
    g2_in,
    g2y_out,
    g2y_in,
    g2z_out,
    g2z_in,
    g2_all,
    g1y_out,
    g1y_in,
    g1z_out,
    g1z_in,
    g1_own,
    g1_all,
    feat_send,
    feat_recv,
    halo_send,
    halo_recv,
    y_send,
    y_recv,
    z_send,
    z_recv,
    cross_send,
    cross_recv,
    load_sems,
    store_sems,
):
    nodes, ny, nz, nf, nb, ns = sizes
    p = lax.axis_index("nodes")
    f = lax.axis_index("feat")
    y, z = p // nz, p % nz
    cols1, cols2 = x_own.shape[1], h_own.shape[1]
    hid = d2.shape[0]
    halo_blocks = x_halo_out.shape[1]
    total = nb + len(OFFSETS) * halo_blocks

    def feat_peer(k):
        return (p, (f + k) % nf)

    def node_peer(offset):
        return ((p + nodes + offset) % nodes, f)

    def y_peer(k):
        return (((y + k) % ny) * nz + z, f)

    def z_peer(k):
        return (y * nz + (z + k) % nz, f)

    def far_first(size):
        return sorted(range(1, size), key=lambda k: -min(k, size - k))

    loads = [
        pltpu.make_async_copy(src, dst, load_sems.at[i])
        for i, (src, dst) in enumerate(
            (
                (x_in, x_ref),
                (lists_in, lists),
                (ids_in, ids),
                (counts_in, counts),
                (adj_in, adj),
                (w1s_in, w1s),
                (w1n_in, w1n),
                (w2s_in, w2s),
                (w2n_in, w2n),
                (up_in, up),
            )
        )
    ]
    for load in loads[:2]:
        load.start()
    stores = [
        pltpu.make_async_copy(src, dst, store_sems.at[i])
        for i, (src, dst) in enumerate(
            (
                (act_o, act_out),
                (fg_o, fg_out),
                (g1s_o, g1s_out),
                (g1n_o, g1n_out),
                (g2s_o, g2s_out),
                (g2n_o, g2n_out),
            )
        )
    ]

    barrier = pltpu.get_barrier_semaphore()
    peers = (
        [z_peer(k) for k in far_first(nz)]
        + [y_peer(k) for k in far_first(ny)]
        + [node_peer(o) for o in OFFSETS]
        + [feat_peer(k) for k in far_first(nf)]
    )
    for peer in peers:
        pl.semaphore_signal(barrier, inc=1, device_id=peer, device_id_type=MESH)
    for s in range(nf):

        @pl.when(jnp.logical_or(f != y, f != s))
        def _():
            pl.semaphore_signal(barrier, inc=1, device_id=(f * nz + z, s), device_id_type=MESH)

    arrivals = len(peers) + ny - jnp.where(f == y, 1, 0)

    sent = []

    def drain():
        while sent:
            sent.pop(0).wait_send()

    def start(src, dst, ssem, rsem, peer):
        copy = pltpu.make_async_remote_copy(
            src_ref=src, dst_ref=dst, send_sem=ssem, recv_sem=rsem, device_id=peer, device_id_type=MESH
        )
        copy.start()
        sent.append(copy)
        return copy

    def feat_hop(hop, src_of, dst):
        copies = []
        for k in far_first(nf):
            g = (f + k) % nf
            copies.append(
                start(src_of(g), dst, feat_send.at[hop, k - 1], feat_recv.at[hop, k - 1], feat_peer(k))
            )
        return copies

    def halo_hop(hop, src, dst_of, sign):
        return [
            start(src.at[i], dst_of(i), halo_send.at[hop, i], halo_recv.at[hop, i], node_peer(sign * o))
            for i, o in sorted(enumerate(OFFSETS), key=lambda pair: -abs(pair[1]))
        ]

    def line_hop(hop, size, src_of, dst, sems, peer_of, me):
        return [
            start(src_of((me + k) % size), dst, sems[0].at[hop, k - 1], sems[1].at[hop, k - 1], peer_of(k))
            for k in far_first(size)
        ]

    def landed(copies):
        for copy in reversed(copies):
            copy.wait_recv()

    loads[0].wait()
    loads[1].wait()
    sent_ids = [[lists[0, h, i] for h in range(halo_blocks)] for i in range(len(OFFSETS))]
    for b in range(nb):
        x_own[b] = x_ref[:, 128 * b : 128 * (b + 1)]
    for i in range(len(OFFSETS)):
        for h in range(halo_blocks):
            x_halo_out[i, h] = x_own[sent_ids[i][h]]

    pl.semaphore_wait(barrier, arrivals)

    halo1 = halo_hop(0, x_halo_out, lambda i: src1.at[pl.ds(nb + halo_blocks * i, halo_blocks)], 1)
    x_all = feat_hop(0, lambda g: x_own, r1.at[:, f, 0])
    for load in loads[2:]:
        load.start()

    src1[pl.ds(0, nb)] = x_own[...]
    src1[total] = jnp.zeros((cols1, 128), BF16)
    src2[total] = jnp.zeros((cols2, 128), BF16)
    r1[:, f, 0] = x_own[...]
    for load in loads[2:5]:
        load.wait()
    targets = [
        [jnp.where(j < counts[b], ids[j, b], total) for j in range(ns)] for b in range(nb)
    ]
    for b in range(nb):
        ones = jnp.concatenate(
            [
                jnp.full((16, 128), jnp.where(targets[b][j] < total, 1.0, 0.0), F32)
                for j in range(ns)
            ],
            1,
        ).astype(BF16)
        deg = sum(mm(ones[:, 128 * j : 128 * (j + 1)], adj[b, j], NT) for j in range(ns))
        rdeg[b] = 1.0 / deg[0:8]
    for load in loads[5:]:
        load.wait()
    for g in range(nf):
        w1i[g, 0:cols1] = w1s[cols1 * g : cols1 * (g + 1)]
        w1i[g, cols1:] = w1n[cols1 * g : cols1 * (g + 1)]
    w1t[...] = w1i[...].reshape(2 * nf * cols1, hid).T.reshape(w1t.shape)

    def aggregate(src, out):
        for b in range(nb):
            total_b = sum(mm(src[targets[b][j]], adj[b, j], NT) for j in range(ns))
            out[b] = (total_b * rdeg[b][0:1]).astype(BF16)

    def dense(out, first, low, high):
        def body(b, carry):
            rows = pl.ds(pl.multiple_of(b * 128, 128), 128)
            for n in range(nb):
                tile = jnp.zeros((8, 16, 128), BF16)
                for j in range(ns):
                    here = jnp.logical_and(j < counts[b], ids[j, b] == first + n)
                    mask = jnp.full((16, 128), jnp.where(here, 1.0, 0.0), F32).astype(BF16)
                    tile = tile + adj[b, j].reshape(8, 16, 128) * mask[None]
                out[rows, 128 * n : 128 * (n + 1)] = tile.reshape(128, 128)
            return carry

        lax.fori_loop(low, high, body, 0)

    def all_blocks(u, lo, c):
        return jnp.concatenate([u[b][lo : lo + c] for b in range(nb)], 1)

    def halo_sums(u, out, c):
        sums = mm(u, to_halo[...]).astype(BF16)
        for n in range(len(OFFSETS) * halo_blocks):
            out[n // halo_blocks, n % halo_blocks] = sums[:, 128 * n : 128 * (n + 1)]

    def with_returned(back, n, c):
        acc = part[0:c, 128 * n : 128 * (n + 1)]
        for i in range(len(OFFSETS)):
            for h in range(halo_blocks):
                here = jnp.where(sent_ids[i][h] == n, 1.0, 0.0)
                acc = acc + here * back[i, h].astype(F32)
        return acc

    landed(halo1)
    aggregate(src1, agg1_col)
    agg1_all = feat_hop(1, lambda g: agg1_col, r1.at[:, f, 1])
    r1[:, f, 1] = agg1_col[...]
    dense(to_halo, nb, 0, nb // 2)
    w2t[:, 0:hid] = w2s[...].T
    w2t[:, hid:] = w2n[...].T
    up_t[...] = up[...].T
    landed(x_all)
    landed(agg1_all)
    blocks1 = [r1[b].reshape(2 * nf * cols1, 128) for b in range(nb)]
    first_cols = mm(w1t[f], jnp.concatenate(blocks1, 1))
    gate = jax.nn.sigmoid(first_cols)
    hidden_cols = (first_cols * gate).astype(BF16)
    for b in range(nb):
        h_own[b] = hidden_cols[:, 128 * b : 128 * (b + 1)]
    for i in range(len(OFFSETS)):
        for h in range(halo_blocks):
            h_halo_out[i, h] = h_own[sent_ids[i][h]]
    halo2 = halo_hop(1, h_halo_out, lambda i: src2.at[pl.ds(nb + halo_blocks * i, halo_blocks)], 1)
    slopes = slope_of(first_cols, gate)
    for b in range(nb):
        slope1_col[b] = slopes[:, 128 * b : 128 * (b + 1)]
    for i in range(len(OFFSETS)):
        for h in range(halo_blocks):
            slope_halo_out[i, h] = slope1_col[sent_ids[i][h]].astype(BF16)
            r1_halo_out[i, h] = r1[sent_ids[i][h]]
    slope_halo = halo_hop(4, slope_halo_out, lambda i: slope_halo_in.at[i], 1)
    r1_halo = halo_hop(5, r1_halo_out, lambda i: r1_halo_in.at[i], 1)
    first_pre = mm(w1t[...].reshape(hid, 2 * nf * cols1), r1[f].reshape(2 * nf * cols1, 128))
    gate = jax.nn.sigmoid(first_pre)
    row2[0:nf] = (first_pre * gate).astype(BF16).reshape(nf, cols2, 128)
    slope1[...] = slope_of(first_pre, gate)
    dense(to_halo, nb, nb // 2, nb)

    src2[pl.ds(0, nb)] = h_own[...]
    landed(halo2)
    aggregate(src2, agg2_col)
    agg2_rows = feat_hop(2, lambda g: agg2_col.at[g], row2.at[nf + f])
    row2[nf + f] = agg2_col[f]
    dense(to_own, 0, 0, nb // 2)
    landed(agg2_rows)
    rows2 = row2[...].reshape(2 * hid, 128)
    second_pre = mm(w2t[...], rows2)
    gate = jax.nn.sigmoid(second_pre)
    delta_two = (up_t[...].astype(F32) * slope_of(second_pre, gate)).astype(BF16)
    d2[...] = delta_two
    own_rdeg = rdeg[f][0:1]
    u2_row[:, 0:cols2] = (mm(w2n[...], delta_two) * own_rdeg).astype(BF16).reshape(nf, cols2, 128)
    self_two = mm(w2s[...], delta_two).astype(BF16)
    self2[...] = self_two
    u2_row[:, cols2:] = self_two.reshape(nf, cols2, 128)
    u2_cols = feat_hop(3, lambda g: u2_row.at[g], u2_col.at[f])
    u2_col[f] = u2_row[f]

    grad2 = mm(rows2, delta_two, NT).astype(BF16)
    g2_out[:, 0:cols2] = grad2[0:hid].reshape(nf, cols2, hid)
    g2_out[:, cols2:] = grad2[hid:].reshape(nf, cols2, hid)
    g2_feat = feat_hop(4, lambda g: g2_out.at[g], g2_in.at[f])
    g2_in[f] = g2_out[f]
    act_o[...] = (second_pre * gate).T.astype(BF16)
    stores[0].start()
    dense(to_own, 0, nb // 2, nb)

    landed(u2_cols)
    u2_all = all_blocks(u2_col, 0, cols2)
    halo_sums(u2_all, back2_out, cols2)
    back2 = halo_hop(2, back2_out, lambda i: back2_in.at[i], -1)
    part[...] = mm(u2_all, to_own[...])

    landed(slope_halo)
    landed(r1_halo)
    deltas, rows = [], []
    for n in range(nb):
        hidden_grad = u2_col[n][cols2:].astype(F32) + part[:, 128 * n : 128 * (n + 1)]
        deltas.append((hidden_grad * slope1_col[n]).astype(BF16))
        rows.append(r1[n].reshape(2 * nf * cols1, 128))
    for i in range(len(OFFSETS)):
        for h in range(halo_blocks):
            returned = back2_out[i, h].astype(F32) * slope_halo_in[i, h].astype(F32)
            deltas.append(returned.astype(BF16))
            rows.append(r1_halo_in[i, h].reshape(2 * nf * cols1, 128))
    copies = 128 // cols2
    grad1 = mm(
        jnp.concatenate(rows, 1), jnp.concatenate([jnp.concatenate(deltas, 1)] * copies, 0), NT
    )
    group = lax.broadcasted_iota(jnp.int32, (8, 128), 1) // cols2
    for g in range(nf):
        packed = jnp.zeros((8, 128), F32)
        for q in range(copies):
            row = 2 * cols1 * g + 8 * q
            packed = jnp.where(group == q, grad1[row : row + 8], packed)
        g1y_out[g] = packed
    y_sems, z_sems = (y_send, y_recv), (z_send, z_recv)
    g1_y = line_hop(1, ny, lambda g: g1y_out.at[g], g1y_in.at[y], y_sems, y_peer, y)
    g1y_in[y] = g1y_out[y]

    landed(g2_feat)
    g2_sum = g2_in[0].astype(F32)
    for k in range(1, nf):
        g2_sum = g2_sum + g2_in[k].astype(F32)
    for g in range(ny):
        for a in range(hid // 128):
            chunk = g2_sum[8 * g : 8 * (g + 1), 128 * a : 128 * (a + 1)]
            g2y_out[g, 8 * a : 8 * (a + 1)] = chunk.astype(BF16)
    g2_y = line_hop(0, ny, lambda g: g2y_out.at[g], g2y_in.at[y], y_sems, y_peer, y)
    g2y_in[y] = g2y_out[y]

    landed(back2)
    for n in range(nb):
        sp2_col[n] = with_returned(back2_in, n, cols2).astype(BF16)
    sp2_rows = feat_hop(5, lambda g: sp2_col.at[g], sp2_row.at[f])
    sp2_row[f] = sp2_col[f]

    landed(g1_y)
    g1z_out[...] = jnp.sum(g1y_in[...], 0)
    g1_z = line_hop(1, nz, lambda g: g1z_out, g1z_in.at[z], z_sems, z_peer, z)
    g1z_in[z] = g1z_out[...]

    landed(g2_y)
    g2z_out[...] = jnp.sum(g2y_in[...].astype(F32), 0).astype(BF16)
    g2_z = line_hop(0, nz, lambda g: g2z_out, g2z_in.at[z], z_sems, z_peer, z)
    g2z_in[z] = g2z_out[...]

    landed(sp2_rows)
    hidden_grad = (
        self2[...].astype(F32) + sp2_row[...].reshape(hid, 128).astype(F32)
    ).astype(BF16)
    delta_one = (hidden_grad.astype(F32) * slope1[...]).astype(BF16)
    back = mm(w1i[...].reshape(2 * nf * cols1, hid), delta_one).reshape(nf, 2 * cols1, 128)
    u1_row[:, 0:cols1] = back[:, 0:cols1].astype(BF16)
    u1_row[:, cols1:] = (back[:, cols1:] * own_rdeg).astype(BF16)
    u1_cols = feat_hop(6, lambda g: u1_row.at[g], u1_col.at[f])
    u1_col[f] = u1_row[f]

    drain()
    landed(u1_cols)
    u1_all = all_blocks(u1_col, cols1, cols1)
    halo_sums(u1_all, back1_out, cols1)
    back1 = halo_hop(3, back1_out, lambda i: back1_in.at[i], -1)
    part[0:cols1] = mm(u1_all, to_own[...])

    landed(g1_z)
    g1_own[...] = jnp.sum(g1z_in[...], 0) * scale
    cross = [
        pltpu.make_async_remote_copy(
            src_ref=g1_own,
            dst_ref=g1_all.at[f],
            send_sem=cross_send.at[k],
            recv_sem=cross_recv.at[f],
            device_id=(((y + k) % ny) * nz + z, y),
            device_id_type=MESH,
        )
        for k in range(ny)
    ]
    for k in far_first(ny):
        cross[k].start()

    @pl.when(f != y)
    def _():
        cross[0].start()

    @pl.when(f == y)
    def _():
        g1_all[f] = g1_own[...]

    landed(g2_z)
    g2_all[y] = (jnp.sum(g2z_in[...].astype(F32), 0) * scale).astype(BF16)
    g2_back = line_hop(2, ny, lambda g: g2_all.at[y], g2_all.at[y], y_sems, y_peer, y)

    landed(back1)
    for n in range(nb):
        fg_o[:, 128 * n : 128 * (n + 1)] = (
            u1_col[n][0:cols1].astype(F32) + with_returned(back1_in, n, cols1)
        ).astype(BF16)
    stores[1].start()

    landed(g2_back)
    for g in range(ny):
        out = g2s_o if 8 * g < cols2 else g2n_o
        row = 8 * g % cols2
        chunk = g2_all[g].astype(F32)
        for a in range(hid // 128):
            out[row : row + 8, 128 * a : 128 * (a + 1)] = chunk[8 * a : 8 * (a + 1)]
    stores[4].start()
    stores[5].start()

    drain()
    for s in range(nf):

        @pl.when(jnp.logical_or(f != y, f != s))
        def _():
            pltpu.make_async_remote_copy(
                src_ref=g1_own,
                dst_ref=g1_all.at[s],
                send_sem=cross_send.at[0],
                recv_sem=cross_recv.at[s],
                device_id=(f * nz + z, s),
                device_id_type=MESH,
            ).wait_recv()

    for q in range(copies):
        out = g1s_o if 8 * q < cols1 else g1n_o
        row = 8 * q % cols1
        for a in range(hid // 128):
            wide = jnp.zeros((8, 128), F32)
            for t in range(copies):
                tile = g1_all[a * copies + t]
                shift = (t - q) * cols2 % 128
                wide = jnp.where(group == t, pltpu.roll(tile, shift, 1) if shift else tile, wide)
            out[row : row + 8, 128 * a : 128 * (a + 1)] = wide
    stores[2].start()
    stores[3].start()

    for k in range(1, ny):
        cross[k].wait_send()

    @pl.when(f != y)
    def _():
        cross[0].wait_send()

    for copy in stores:
        copy.wait()


def store(count, *refs):
    ins, outs, held = refs[:count], refs[count : 2 * count], refs[2 * count : 3 * count]
    sems = refs[-1]
    fetch = [pltpu.make_async_copy(ins[i], held[i], sems.at[0, i]) for i in range(count)]
    write = [pltpu.make_async_copy(held[i], outs[i], sems.at[1, i]) for i in range(count)]
    for copy in fetch:
        copy.start()
    for first, second in zip(fetch, write):
        first.wait()
        second.start()
    for copy in write:
        copy.wait()


def on_device(
    features,
    adjacency,
    source_ids,
    counts,
    send_lists,
    first_self,
    first_neighbour,
    second_self,
    second_neighbour,
    upstream,
):
    nodes, nf = lax.axis_size("nodes"), lax.axis_size("feat")
    ny = 8
    nz = nodes // ny
    nb, ns, bs = adjacency.shape[0], adjacency.shape[1], adjacency.shape[2]
    hs = send_lists.shape[2]
    total = nb + len(OFFSETS) * hs
    c1 = features.shape[1]
    hid = upstream.shape[1]
    c2 = hid // nf
    noff = len(OFFSETS)
    scale = 1.0 / math.sqrt(nb * bs * nodes)
    hbm = pl.BlockSpec(memory_space=pltpu.HBM)
    scratch = [
        ((bs, hid), BF16),
        ((c1, nb * bs), BF16),
        ((c1, hid), F32),
        ((c1, hid), F32),
        ((c2, hid), F32),
        ((c2, hid), F32),
        ((c1, nb * bs), BF16),
        (adjacency.shape, BF16),
        (first_self.shape, BF16),
        (first_neighbour.shape, BF16),
        (second_self.shape, BF16),
        (second_neighbour.shape, BF16),
        (upstream.shape, BF16),
        ((nf, 2 * c1, hid), BF16),
        ((nf, c2, 2 * nf * c1), BF16),
        ((hid, 2 * hid), BF16),
        ((hid, bs), BF16),
        ((nb, 8, bs), F32),
        ((nb, c1, bs), BF16),
        ((noff, hs, c1, bs), BF16),
        ((total + 1, c1, bs), BF16),
        ((nb, c1, bs), BF16),
        ((nb, nf, 2, c1, bs), BF16),
        ((hid, bs), F32),
        ((nb, c2, bs), F32),
        ((noff, hs, c2, bs), BF16),
        ((noff, hs, c2, bs), BF16),
        ((noff, hs, nf, 2, c1, bs), BF16),
        ((noff, hs, nf, 2, c1, bs), BF16),
        ((2 * nf, c2, bs), BF16),
        ((nb, c2, bs), BF16),
        ((noff, hs, c2, bs), BF16),
        ((total + 1, c2, bs), BF16),
        ((nb, c2, bs), BF16),
        ((hid, bs), BF16),
        ((hid, bs), BF16),
        ((nf, 2 * c2, bs), BF16),
        ((nb, 2 * c2, bs), BF16),
        ((nb * bs, noff * hs * bs), BF16),
        ((nb * bs, nb * bs), BF16),
        ((c2, nb * bs), F32),
        ((noff, hs, c2, bs), BF16),
        ((noff, hs, c2, bs), BF16),
        ((nb, c2, bs), BF16),
        ((nf, c2, bs), BF16),
        ((nf, 2 * c1, bs), BF16),
        ((nb, 2 * c1, bs), BF16),
        ((noff, hs, c1, bs), BF16),
        ((noff, hs, c1, bs), BF16),
        ((nf, 2 * c2, hid), BF16),
        ((nf, 2 * c2, hid), BF16),
        ((ny, 16, 128), BF16),
        ((ny, 16, 128), BF16),
        ((16, 128), BF16),
        ((nz, 16, 128), BF16),
        ((ny, 16, 128), BF16),
        ((ny, 8, 128), F32),
        ((ny, 8, 128), F32),
        ((8, 128), F32),
        ((nz, 8, 128), F32),
        ((8, 128), F32),
        ((nf, 8, 128), F32),
    ]
    dma = pltpu.SemaphoreType.DMA
    outs = pl.pallas_call(
        functools.partial(kernel, (nodes, ny, nz, nf, nb, ns), scale),
        out_shape=(
            jax.ShapeDtypeStruct((bs, hid), BF16),
            jax.ShapeDtypeStruct((c1, nb * bs), BF16),
            jax.ShapeDtypeStruct((c1, hid), F32),
            jax.ShapeDtypeStruct((c1, hid), F32),
            jax.ShapeDtypeStruct((c2, hid), F32),
            jax.ShapeDtypeStruct((c2, hid), F32),
        ),
        in_specs=[hbm] * 10,
        out_specs=(hbm,) * 6,
        scratch_shapes=[pltpu.VMEM(shape, kind) for shape, kind in scratch[:6]]
        + [
            pltpu.SMEM((ns, nb), jnp.int32),
            pltpu.SMEM((nb,), jnp.int32),
            pltpu.SMEM((1, hs, noff), jnp.int32),
        ]
        + [pltpu.VMEM(shape, kind) for shape, kind in scratch[6:]]
        + [
            dma((7, nf - 1)),
            dma((7, nf - 1)),
            dma((6, noff)),
            dma((6, noff)),
            dma((3, ny - 1)),
            dma((3, ny - 1)),
            dma((2, nz - 1)),
            dma((2, nz - 1)),
            dma((ny,)),
            dma((nf,)),
            dma((10,)),
            dma((6,)),
        ],
        compiler_params=pltpu.CompilerParams(
            collective_id=0, has_side_effects=True, vmem_limit_bytes=60 * 1024 * 1024
        ),
    )(
        source_ids.T,
        counts,
        send_lists.transpose(0, 2, 1),
        features.T,
        adjacency,
        first_self,
        first_neighbour,
        second_self,
        second_neighbour,
        upstream,
    )
    outs = pl.pallas_call(
        functools.partial(store, len(outs)),
        out_shape=tuple(jax.ShapeDtypeStruct(o.shape, o.dtype) for o in outs),
        in_specs=[hbm] * len(outs),
        out_specs=(hbm,) * len(outs),
        scratch_shapes=[pltpu.VMEM(o.shape, o.dtype) for o in outs] + [dma((2, len(outs)))],
        compiler_params=pltpu.CompilerParams(vmem_limit_bytes=60 * 1024 * 1024),
    )(*outs)
    return (outs[0], outs[1].T) + tuple(outs[2:])


def solution(mesh):
    return jax.shard_map(
        on_device,
        mesh=mesh,
        in_specs=(
            P("nodes", "feat"),
            P("nodes", None, None, None),
            P("nodes", None),
            P("nodes"),
            P("nodes", None, None),
            P(),
            P(),
            P(),
            P(),
            P(("nodes", "feat"), None),
        ),
        out_specs=(
            P(("nodes", "feat"), None),
            P("nodes", "feat"),
            P("feat", None),
            P("feat", None),
            P("feat", None),
            P("feat", None),
        ),
        check_vma=False,
    )
```
